256 devices in a mesh: seq: 64 (over y, z, core), chan: 4 (over x).
Axes of the slice: x: 4, y: 4, z: 8, core: 2. Of those that a mesh axis runs over, the one named last changes fastest.
Arguments:
- inputs: bfloat16 [32768, 1536], P('seq', 'chan'), may hold values from -16 to 16
- conv_weight: bfloat16 [1, 3, 1536, 1536], P(None, None, None, 'chan'), may hold values from -0.09375 to 0.09375
- head_weight: bfloat16 [1536, 4096], P(None, 'chan'), may hold values from -0.15625 to 0.15625
- head_cot: bfloat16 [32768, 4096], P('seq', 'chan'), may hold values from -6 to 6
- exon_blocks: int32 [512, 8], P('seq'), may hold values from 0 to 255
Outputs:
- tracks: bfloat16 [32768, 4096], P('seq', 'chan')
- coverage: float32 [512, 4096], P('seq', 'chan')
- input_grad: bfloat16 [32768, 1536], P('seq', 'chan')
- kernel_gradient: float32 [1, 3, 1536, 1536], P(None, None, 'seq', 'chan')
The draws below stay inside these ranges and needn't reach their ends.
All inputs are finite; a program needn't handle non-finite values.
Results may differ from the reference program's by a relative error of at most 0.0059.
Values may be sent and summed in bfloat16 or wider, within the bound.
No kernel may reach another device: no remote copies, remote signals or barrier semaphores. Data moves between devices by JAX's collectives and lax.ppermute only.
A program may use at most 64 MiB of HBM per device.

```python
import jax
import jax.numpy as jnp

C = 1536
LAYERS = 1
BLOCK = 128
EXONS = 8
BASE_DILATION = 1024
BINS = 32768
BLOCKS = 256
TRACKS = 4096
GENES = 512


def set_ends(result, own_key, smallest, largest):
    index_at = [jax.random.randint(jax.random.fold_in(own_key, axis), (), 0, length) for axis, length in enumerate(result.shape)]
    widest = result.shape.index(max(result.shape))
    beside = index_at[:widest] + [(index_at[widest] + 1) % result.shape[widest]] + index_at[widest + 1:]
    return result.at[tuple(index_at)].set(smallest).at[tuple(beside)].set(largest)


def with_spikes(drawn, key, source, target, shards_of, factor):
    owner, partner = [(jnp.arange(drawn.shape[dim]) // (drawn.shape[dim] // shards_of)).reshape([-1 if axis == dim else 1 for axis in range(drawn.ndim)]) for dim in (source, target)]
    chosen = jax.random.permutation(key, shards_of)[partner]
    strong = (owner == chosen) | (owner == (partner + shards_of // 2) % shards_of)
    return jnp.where(strong, factor * drawn, drawn)


def block_scale(key, shape, cuts, smallest, largest):
    def one(axis_at, shards_of):
        draws = jax.random.uniform(jax.random.fold_in(jax.random.fold_in(key, 6), axis_at), (shards_of,), jnp.float32, smallest / len(cuts), largest / len(cuts))
        return jnp.repeat(jnp.exp(draws), shape[axis_at] // shards_of).reshape((-1,) + (1,) * (len(shape) - axis_at - 1))

    gain = one(*cuts[0])
    for cut in cuts[1:]:
        gain = gain * one(*cut)
    return gain


def bell_draw(rng, shape, scale, most, shards=(), held_as=jnp.bfloat16):
    gain = block_scale(rng, shape, shards, -0.22, 0.18) if shards else 1.0
    result = jax.random.normal(rng, shape, jnp.float32) * scale * gain
    return jnp.minimum(jnp.maximum(result, -most), most).astype(held_as)


def gaussian_with(own_key, dims, spread, most, split, heavy, kind=jnp.bfloat16):
    result = spread * jax.random.normal(own_key, dims, jnp.float32)
    if split:
        result = result * block_scale(own_key, dims, split, -0.22, 0.18)
    return jnp.clip(with_spikes(result, jax.random.fold_in(own_key, 3), *heavy), -most, most).astype(kind)


def setup_inputs(seed: int = 0) -> dict:
    seeds = jax.random.split(jax.random.key(seed), 6)
    return {
        "inputs": gaussian_with(seeds[0], (BINS, C), 1.0, 16.0, ((0, 64), (1, 4)), (0, 1, 64, 4.0)),
        "conv_weight": bell_draw(seeds[1], (LAYERS, 3, C, C), (3 * C) ** -0.5, 0.09375, ((3, 4),)),
        "head_weight": bell_draw(seeds[2], (C, TRACKS), C ** -0.5, 0.15625, ((1, 4),)),
        "head_cot": bell_draw(seeds[3], (BINS, TRACKS), 1.0, 6.0, ((0, 64), (1, 4))),
        "exon_blocks": set_ends(jax.random.randint(seeds[4], (GENES, EXONS), 0, BLOCKS), jax.random.fold_in(seeds[4], 1), 0, BLOCKS - 1).astype(jnp.int32),
    }


def move_rows(values, offset):
    count = values.shape[0]
    zeros = jnp.zeros((abs(offset),) + values.shape[1:], values.dtype)
    if offset > 0:
        return jnp.concatenate([values[offset:], zeros], axis=0)
    return jnp.concatenate([zeros, values[:count + offset]], axis=0)

def activation_slope(point, cotan):
    _, back = jax.vjp(jax.nn.gelu, point)
    return back(cotan)[0]

def reference(inputs, conv_weight, head_weight, head_cot, exon_blocks):
    state = inputs
    saved = []
    for layer_number in range(LAYERS):
        receptive_span = BASE_DILATION * 2 ** layer_number
        acted = jax.nn.gelu(state.astype(jnp.float32)).astype(jnp.bfloat16)
        mixed = jnp.dot(move_rows(acted, -receptive_span), conv_weight[layer_number, 0], preferred_element_type=jnp.float32)
        mixed = mixed + jnp.dot(acted, conv_weight[layer_number, 1], preferred_element_type=jnp.float32)
        mixed = mixed + jnp.dot(move_rows(acted, receptive_span), conv_weight[layer_number, 2], preferred_element_type=jnp.float32)
        saved.append((state, acted))
        state = (state.astype(jnp.float32) + mixed).astype(jnp.bfloat16)
    logits = jnp.dot(state, head_weight, preferred_element_type=jnp.float32)
    tracks = jax.nn.softplus(logits).astype(jnp.bfloat16)
    block_partial_sums = tracks.astype(jnp.float32).reshape(BLOCKS, BLOCK, TRACKS).sum(axis=1)
    coverage = block_partial_sums[exon_blocks].sum(axis=1) / jnp.sqrt(jnp.float32(EXONS * BLOCK))
    head_term = (head_cot.astype(jnp.float32) * jax.nn.sigmoid(logits)).astype(jnp.bfloat16)
    grad = jnp.dot(head_term, head_weight.T, preferred_element_type=jnp.float32)
    grads = []
    for layer_number in reversed(range(LAYERS)):
        receptive_span = BASE_DILATION * 2 ** layer_number
        before, acted = saved[layer_number]
        grad_low = grad.astype(jnp.bfloat16)
        later = move_rows(grad_low, receptive_span)
        earlier = move_rows(grad_low, -receptive_span)
        back_u = jnp.dot(later, conv_weight[layer_number, 0].T, preferred_element_type=jnp.float32)
        back_u = back_u + jnp.dot(grad_low, conv_weight[layer_number, 1].T, preferred_element_type=jnp.float32)
        back_u = back_u + jnp.dot(earlier, conv_weight[layer_number, 2].T, preferred_element_type=jnp.float32)
        kernel = jnp.stack([jnp.dot(acted.T, later, preferred_element_type=jnp.float32), jnp.dot(acted.T, grad_low, preferred_element_type=jnp.float32), jnp.dot(acted.T, earlier, preferred_element_type=jnp.float32)])
        grads.append(kernel)
        grad = grad + activation_slope(before.astype(jnp.float32), back_u)
    kernel_gradient = jnp.stack(grads[::-1])
    return (tracks, coverage, grad.astype(jnp.bfloat16), kernel_gradient)
```

```python
import jax
import jax.numpy as jnp
from jax import lax
from jax.sharding import PartitionSpec as P

BLOCK = 128
EXONS = 8
NX, NY, NZ = 4, 4, 8
CHUNKS = 2
F32 = jnp.float32
BF = jnp.bfloat16


def activation_slope(point, cotan):
    _, back = jax.vjp(jax.nn.gelu, point)
    return back(cotan)[0]


def shifted(value, steps):
    count = lax.axis_size("seq")
    leading, last = (max(0, -steps), min(count, count - steps))
    return lax.ppermute(value, "seq", [(s, s + steps) for s in range(leading, last)])


def along_x(value, steps):
    return lax.ppermute(value, "chan", [(i, (i + steps) % NX) for i in range(NX)])


def seq_index(y, z, core):
    return (y * NZ + z) * 2 + core


def along_seq(value, dy, dz, dcore):
    pairs = []
    for y in range(NY):
        for z in range(NZ):
            for core in range(2):
                pairs.append(
                    (
                        seq_index(y, z, core),
                        seq_index((y + dy) % NY, (z + dz) % NZ, (core + dcore) % 2),
                    )
                )
    return lax.ppermute(value, "seq", pairs)


def gather_x(value):
    return jnp.concatenate([value] + [along_x(value, -r) for r in range(1, NX)], axis=1)


def scatter_x(blocks):
    total = blocks[0]
    for r in range(1, NX):
        total = total + along_x(blocks[r].astype(BF), r).astype(F32)
    return total


def times_t(left, right):
    return lax.dot_general(left, right, (((1,), (1,)), ((), ())), preferred_element_type=F32)


def inner_rows(left, right):
    return lax.dot_general(left, right, (((0,), (0,)), ((), ())), preferred_element_type=F32)


def pick(value, index, axis=0):
    return lax.dynamic_index_in_dim(value, index, axis, keepdims=False)


def scatter_kernel(total):
    x = lax.axis_index("chan")
    s = lax.axis_index("seq")
    core, z, y = s % 2, (s // 2) % NZ, s // (2 * NZ)
    cols = total.shape[1]
    total = total.reshape(NY, NZ, 2, 24, cols)
    kept = pick(total, core, 2)
    other = pick(total, 1 - core, 2).astype(BF)
    total = kept + along_seq(other, 0, 0, 1).astype(F32)
    kept = pick(total, (y - x) % NY)
    for m in range(1, NY):
        kept = kept + along_seq(pick(total, (y + m - x) % NY).astype(BF), m, 0, 0).astype(F32)
    total = kept
    kept = pick(total, z)
    for m in range(1, NZ):
        kept = kept + along_seq(pick(total, (z + m) % NZ).astype(BF), 0, m, 0).astype(F32)
    return kept


def exchange(value, flip_y, flip_z, flip_core):
    pairs = []
    for y in range(NY):
        for z in range(NZ):
            for core in range(2):
                pairs.append(
                    (
                        seq_index(y, z, core),
                        seq_index(y ^ flip_y, z ^ flip_z, core ^ flip_core),
                    )
                )
    return lax.ppermute(value, "seq", pairs)


def gather_blocks(value):
    s = lax.axis_index("seq")
    own = value.shape[0]
    flips = jnp.zeros((1,), jnp.int32)
    for flip in ((1, 0, 0), (2, 0, 0), (0, 1, 0), (0, 2, 0), (0, 4, 0), (0, 0, 1)):
        value = jnp.concatenate([value, exchange(value, *flip)], axis=0)
        flips = jnp.concatenate([flips, flips ^ seq_index(*flip)])
    labels = ((s ^ flips) * own)[:, None] + jnp.arange(own, dtype=jnp.int32)[None]
    return value, labels.reshape(-1)


def shards(inputs, conv_weight, head_weight, head_cot, exon_blocks):
    rows, width = inputs.shape
    x = lax.axis_index("chan")
    size = rows // CHUNKS
    steps = 2

    taps = jnp.concatenate([conv_weight[0, k] for k in range(3)], axis=1)
    taps = jnp.roll(taps.reshape(NX, width, 3 * width), -x, axis=0).reshape(NX * width, 3 * width)
    head = jnp.roll(head_weight.reshape(NX, width, -1), -x, axis=0).reshape(NX * width, -1)

    states = [inputs[c * size : (c + 1) * size].astype(F32) for c in range(CHUNKS)]
    wholes, tracks, sums, grads, dzs = [], [], [], [], []
    for c in range(CHUNKS):
        acted = jax.nn.gelu(states[c]).astype(BF)
        whole = gather_x(acted)
        wholes.append(whole)
        products = jnp.dot(whole, taps, preferred_element_type=F32)
        lower = shifted(products[:, :width].astype(BF), steps)
        upper = shifted(products[:, 2 * width :].astype(BF), -steps)
        mixed = products[:, width : 2 * width] + lower.astype(F32) + upper.astype(F32)
        full = gather_x((states[c] + mixed).astype(BF))
        logits = jnp.dot(full, head, preferred_element_type=F32)
        track = jax.nn.softplus(logits).astype(BF)
        tracks.append(track)
        sums.append(track.astype(F32).reshape(size // BLOCK, BLOCK, -1).sum(axis=1))
        cot = head_cot[c * size : (c + 1) * size].astype(F32)
        term = (cot * jax.nn.sigmoid(logits)).astype(BF)
        back = times_t(term, head)
        grads.append(scatter_x([back[:, r * width : (r + 1) * width] for r in range(NX)]))
    outs, kernel = [], None
    for c in range(CHUNKS):
        low = grads[c].astype(BF)
        later = shifted(low, -steps)
        earlier = shifted(low, steps)
        around = jnp.concatenate([later, low, earlier], axis=1)
        back = times_t(around, taps)
        part = inner_rows(wholes[c], around)
        kernel = part if kernel is None else kernel + part
        back_u = scatter_x([back[:, r * width : (r + 1) * width] for r in range(NX)])
        outs.append((grads[c] + activation_slope(states[c], back_u)).astype(BF))
    kernel = scatter_kernel(kernel)
    kernel_gradient = kernel.reshape(24, 3, width).transpose(1, 0, 2)[None]

    all_blocks, labels = gather_blocks(jnp.concatenate(sums, axis=0).astype(BF))
    counts = jnp.sum((exon_blocks[:, :, None] == labels[None, None, :]).astype(F32), axis=1)
    coverage = jnp.dot(counts.astype(BF), all_blocks, preferred_element_type=F32)
    coverage = coverage / jnp.sqrt(F32(EXONS * BLOCK))
    return (jnp.concatenate(tracks, axis=0), coverage, jnp.concatenate(outs, axis=0), kernel_gradient)


def solution(mesh):
    return jax.shard_map(
        shards,
        mesh=mesh,
        in_specs=(
            P("seq", "chan"),
            P(None, None, None, "chan"),
            P(None, "chan"),
            P("seq", "chan"),
            P("seq", None),
        ),
        out_specs=(
            P("seq", "chan"),
            P("seq", "chan"),
            P("seq", "chan"),
            P(None, None, "seq", "chan"),
        ),
        check_vma=False,
    )
```

```python
import jax
import jax.numpy as jnp
from jax import lax
from jax.experimental import pallas as pl
from jax.experimental.pallas import tpu as pltpu
from jax.sharding import PartitionSpec as P

BLOCK = 128
EXONS = 8
NX, NY, NZ = 4, 4, 8
TAPS = 3
GROUP = 24
F32 = jnp.float32
BF = jnp.bfloat16


def activation_slope(point, cotan):
    _, back = jax.vjp(jax.nn.gelu, point)
    return back(cotan)[0]


def seq_index(y, z, core):
    return (y * NZ + z) * 2 + core


def shifted(value, steps):
    count = lax.axis_size("seq")
    leading, last = (max(0, -steps), min(count, count - steps))
    return lax.ppermute(value, "seq", [(s, s + steps) for s in range(leading, last)])


def along_x(value, steps):
    return lax.ppermute(value, "chan", [(i, (i + steps) % NX) for i in range(NX)])


def along_seq(value, dy, dz, dcore):
    pairs = [
        (
            seq_index(y, z, core),
            seq_index((y + dy) % NY, (z + dz) % NZ, (core + dcore) % 2),
        )
        for y in range(NY)
        for z in range(NZ)
        for core in range(2)
    ]
    return lax.ppermute(value, "seq", pairs)


def from_all_x(value):
    return [value] + [along_x(value, -r) for r in range(1, NX)]


def times_t(left, right):
    return lax.dot_general(left, right, (((1,), (1,)), ((), ())), preferred_element_type=F32)


def call(body, place, operands, outs, scratch=(), after=(), limit=56, flops=0, moved=0):
    count = len(operands)

    def kernel(*refs):
        body(refs[0], *refs[1 : 1 + count], *refs[1 + count + len(after) :])

    vmem = pl.BlockSpec(memory_space=pltpu.VMEM)
    return pl.pallas_call(
        kernel,
        in_specs=[pl.BlockSpec(memory_space=pltpu.SMEM)]
        + [pl.BlockSpec(memory_space=space) for _, space in operands]
        + [pl.BlockSpec(memory_space=pl.ANY)] * len(after),
        out_specs=[vmem] * len(outs),
        scratch_shapes=list(scratch),
        out_shape=outs,
        cost_estimate=pl.CostEstimate(flops=flops, bytes_accessed=moved, transcendentals=0),
        compiler_params=pltpu.CompilerParams(vmem_limit_bytes=limit * 2**20),
    )(place, *[value for value, _ in operands], *after)


def local(values):
    return [(value, pltpu.VMEM) for value in values]


def like(shape, dtype):
    return jax.ShapeDtypeStruct(shape, dtype)


def slot(place, r, width):
    return pl.ds(pl.multiple_of(lax.rem(place[0] + r, NX) * width, 128), width)


def outer_products(place, blocks, conv_weight, after):
    size, width = blocks[0].shape
    tall = NX * width

    def body(place, b0, b1, b2, b3, weight, low, up, whole, held, sems):
        copies = [
            pltpu.make_async_copy(weight.at[0, tap], held.at[i], sems.at[i])
            for i, tap in enumerate((0, 2))
        ]
        for copy in copies:
            copy.start()
        for r, block in enumerate((b0, b1, b2, b3)):
            whole[:, slot(place, r, width)] = block[...]
        for i, ref in enumerate((low, up)):
            copies[i].wait()
            ref[...] = jnp.dot(whole[...], held[i], preferred_element_type=F32).astype(BF)

    block = (size, width)
    return call(
        body,
        place,
        local(blocks) + [(conv_weight, pl.ANY)],
        [like(block, BF), like(block, BF), like((size, tall), BF)],
        scratch=[pltpu.VMEM((2, tall, width), BF), pltpu.SemaphoreType.DMA((2,))],
        after=after,
        flops=4 * size * tall * width,
        moved=4 * tall * width,
    )


def turned_blocks(place, whole, after):
    size, tall = whole.shape
    width = tall // NY

    def body(place, whole, *outs):
        for m, out in enumerate(outs):
            at = pl.multiple_of(lax.rem(place[1] + m, NY) * width, 128)
            out[...] = whole[:, pl.ds(at, width)].T

    return call(
        body,
        place,
        local([whole]),
        [like((width, size), BF)] * NY,
        after=after,
        flops=size * tall,
        moved=4 * size * tall,
    )


def middle_product(place, whole, conv_weight, after):
    size, tall = whole.shape
    width = tall // NX

    def body(place, whole, weight, mid, held, sem):
        copy = pltpu.make_async_copy(weight.at[0, 1], held, sem)
        copy.start()
        copy.wait()
        mid[...] = jnp.dot(whole[...], held[...], preferred_element_type=F32)

    return call(
        body,
        place,
        local([whole]) + [(conv_weight, pl.ANY)],
        [like((size, width), F32)],
        scratch=[pltpu.VMEM((tall, width), BF), pltpu.SemaphoreType.DMA(())],
        after=after,
        flops=2 * size * tall * width,
        moved=2 * tall * width,
    )[0]


def track_head(place, blocks, head_weight, head_cot, after):
    size, width = blocks[0].shape
    tall, wide = head_weight.shape
    tile = 256
    groups = size // BLOCK

    def body(place, b0, b1, b2, b3, weight, cot, out, sums, o0, o1, o2, o3, whole, held, term, cots, sems):
        copies = []
        for j in range(wide // tile):
            cols = slice(j * tile, (j + 1) * tile)
            copies.append(
                (
                    pltpu.make_async_copy(weight.at[:, cols], held.at[:, cols], sems.at[0, j]),
                    pltpu.make_async_copy(cot.at[:, cols], cots.at[:, cols], sems.at[1, j]),
                )
            )
            for copy in copies[-1]:
                copy.start()
        for r, block in enumerate((b0, b1, b2, b3)):
            whole[:, slot(place, r, width)] = block[...]
        for j in range(wide // tile):
            cols = slice(j * tile, (j + 1) * tile)
            for copy in copies[j]:
                copy.wait()
            logits = jnp.dot(whole[...], held[:, cols], preferred_element_type=F32)
            decay = jnp.exp(-jnp.abs(logits))
            track = (jnp.maximum(logits, 0.0) + jnp.log1p(decay)).astype(BF)
            out[:, cols] = track
            sums[:, cols] = jnp.sum(track.astype(F32).reshape(groups, BLOCK, tile), axis=1)
            sigmoid = jnp.where(logits >= 0.0, 1.0, decay) / (1.0 + decay)
            term[:, cols] = (cots[:, cols].astype(F32) * sigmoid).astype(BF)
        for r, ref in ((2, o2), (1, o1), (3, o3), (0, o0)):
            ref[...] = times_t(term[...], held[slot(place, r, width), :]).astype(ref.dtype)

    block = (size, width)
    return call(
        body,
        place,
        local(blocks) + [(head_weight, pl.ANY), (head_cot, pl.ANY)],
        [like((size, wide), BF), like((groups, wide), F32), like(block, F32)] + [like(block, BF)] * 3,
        scratch=[
            pltpu.VMEM((size, tall), BF),
            pltpu.VMEM((tall, wide), BF),
            pltpu.VMEM((size, wide), BF),
            pltpu.VMEM((size, wide), BF),
            pltpu.SemaphoreType.DMA((2, wide // tile)),
        ],
        after=after,
        flops=4 * size * tall * wide,
        moved=2 * tall * wide,
    )


def add_up(place, own, came, after):
    def body(place, own, c1, c2, c3, total, low):
        value = own[...] + c1[...].astype(F32) + c2[...].astype(F32) + c3[...].astype(F32)
        total[...] = value
        low[...] = value.astype(BF)

    shape = own.shape
    return call(
        body,
        place,
        local([own] + came),
        [like(shape, F32), like(shape, BF)],
        after=after,
        flops=4 * own.size,
        moved=16 * own.size,
    )


def back_products(place, around, conv_weight, after):
    size, width = around[0].shape
    tall = NX * width
    cols = TAPS * width

    def body(place, d0, d1, d2, weight, o0, o1, o2, o3, held, joined, sems):
        copies = []
        for k in range(TAPS):
            at = slice(k * width, (k + 1) * width)
            copies.append(pltpu.make_async_copy(weight.at[0, k], held.at[:, at], sems.at[k]))
            copies[-1].start()
        for k, ref in enumerate((d0, d1, d2)):
            joined[:, k * width : (k + 1) * width] = ref[...]
        for copy in copies:
            copy.wait()
        for r, ref in ((2, o2), (1, o1), (3, o3), (0, o0)):
            ref[...] = times_t(joined[...], held[slot(place, r, width), :]).astype(ref.dtype)

    block = (size, width)
    return call(
        body,
        place,
        local(around) + [(conv_weight, pl.ANY)],
        [like(block, F32)] + [like(block, BF)] * 3,
        scratch=[
            pltpu.VMEM((tall, cols), BF),
            pltpu.VMEM((size, cols), BF),
            pltpu.SemaphoreType.DMA((TAPS,)),
        ],
        after=after,
        flops=2 * size * tall * cols,
        moved=2 * tall * cols,
    )


def kernel_terms(place, earlier, own, later, cots, after):
    _, width, size = own.shape
    half = width // 2
    cols = TAPS * width

    def body(place, earlier, own, later, d0, d1, d2, d3, kept, sent):
        y, z, core = place[1], place[2], place[3]
        first, last = z == 0, z == NZ - 1
        for k, left in enumerate((earlier, own, later)):
            total = jnp.zeros((width, width), F32)
            for m, right in enumerate((d0, d1, d2, d3)):
                if k == 0:
                    index = jnp.where(first, (m + 1) % NY, m)
                    valid = jnp.logical_not(jnp.logical_and(first, y == m))
                elif k == 2:
                    index = jnp.where(last, (m + NY - 1) % NY, m)
                    valid = jnp.logical_not(jnp.logical_and(last, y == (m + NY - 1) % NY))
                else:
                    index, valid = m, None
                product = jnp.dot(left[index], right[...], preferred_element_type=F32)
                total += product if valid is None else jnp.where(valid, product, 0.0)
            pairs = total.reshape(half // GROUP, 2, GROUP, width)
            one, two = (pairs[:, i].reshape(half, width) for i in range(2))
            at = slice(k * width, (k + 1) * width)
            kept[:, at] = jnp.where(core == 0, one, two)
            sent[:, at] = jnp.where(core == 0, two, one).astype(BF)

    return call(
        body,
        place,
        local([earlier, own, later] + cots),
        [like((half, cols), F32), like((half, cols), BF)],
        after=after,
        flops=2 * size * NY * width * cols,
        moved=8 * NY * width * size,
    )


def over_z(place, kept, came, after):
    rows, cols = kept.shape

    def body(place, kept, came, *refs):
        outs, total = refs[:NZ], refs[NZ]
        total[...] = kept[...] + came[...].astype(F32)
        for m, ref in enumerate(outs):
            at = pl.multiple_of(lax.rem(place[2] + m, NZ) * GROUP, 8)
            ref[...] = total[pl.ds(at, GROUP), :].astype(ref.dtype)

    block = (GROUP, cols)
    return call(
        body,
        place,
        local([kept, came]),
        [like(block, F32)] + [like(block, BF)] * (NZ - 1),
        scratch=[pltpu.VMEM((rows, cols), F32)],
        after=after,
        limit=16,
        flops=4 * rows * cols,
        moved=6 * rows * cols,
    )


def coverage_of(blocks, order, exon_blocks):
    count, lines, half = blocks.shape
    own = lines // 2
    line = jnp.arange(lines, dtype=jnp.int32)
    labels = order[:, None] * own + line[None] // 2
    hits = (exon_blocks[:, :, None, None] == labels[None, None]).astype(F32).sum(axis=1)
    counts = jnp.stack([jnp.where(line % 2 == side, hits, 0.0) for side in range(2)])
    total = jnp.dot(
        counts.astype(BF).reshape(-1, count * lines),
        blocks.reshape(count * lines, half),
        preferred_element_type=F32,
    )
    total = total.reshape(2, -1, half).transpose(1, 0, 2).reshape(-1, 2 * half)
    return total / jnp.sqrt(F32(EXONS * BLOCK))


def shards(inputs, conv_weight, head_weight, head_cot, exon_blocks):
    width = inputs.shape[1]
    x = lax.axis_index("chan")
    s = lax.axis_index("seq")
    core, z, y = s % 2, (s // 2) % NZ, s // (2 * NZ)
    place = jnp.stack([x, y, z, core]).astype(jnp.int32)
    steps = 2

    state = inputs.astype(F32)
    acted = from_all_x(jax.nn.gelu(state).astype(BF))
    low, up, whole = outer_products(place, acted, conv_weight, ())
    low, up = shifted(low, steps), shifted(up, -steps)
    mid = middle_product(place, whole, conv_weight, ())
    turned = turned_blocks(place, whole, (mid,))
    full = from_all_x((state + (mid + low.astype(F32) + up.astype(F32))).astype(BF))
    turned = jnp.stack([turned[0]] + [along_seq(turned[m], m, 0, 0) for m in range(1, NY)])
    before = along_seq(turned, 0, 1, 0)
    behind = along_seq(turned, 0, NZ - 1, 0)

    tracks, sums, *blocks = track_head(place, full, head_weight, head_cot, (turned,))
    came = [along_x(blocks[r], r) for r in range(1, NX)]
    sums = sums.astype(BF).reshape(1, -1, 512)
    z_groups = [[seq_index(j, i, c) for i in range(NZ)] for j in range(NY) for c in range(2)]
    other_groups = [[seq_index(j, i, c) for j in range(NY) for c in range(2)] for i in range(NZ)]
    sums = lax.all_gather(sums, "seq", axis=0, tiled=True, axis_index_groups=z_groups)
    gathered = lax.all_gather(sums, "seq", axis=0, tiled=True, axis_index_groups=other_groups)
    order = jnp.array([seq_index(j, i, c) for j in range(NY) for c in range(2) for i in range(NZ)], jnp.int32)

    grad, low = add_up(place, blocks[0], came, (before, behind, gathered))
    cots = [low] + [along_seq(low, m, 0, 0) for m in range(1, NY)]
    around = [shifted(low, -steps), low, shifted(low, steps)]
    blocks = back_products(place, around, conv_weight, ())
    came = [along_x(blocks[r], r) for r in range(1, NX)]
    kept, sent = kernel_terms(place, before, turned, behind, cots, (blocks[1],))
    kept, *parts = over_z(place, kept, along_seq(sent, 0, 0, 1), ())
    for m, part in enumerate(parts):
        kept = kept + along_seq(part, 0, m + 1, 0).astype(F32)
    kernel_gradient = kept.reshape(GROUP, TAPS, width).transpose(1, 0, 2)[None]

    back_u = blocks[0] + came[0].astype(F32) + came[1].astype(F32) + came[2].astype(F32)
    out = (grad + activation_slope(state, back_u)).astype(BF)
    coverage = coverage_of(gathered, order, exon_blocks)
    return (tracks, coverage, out, kernel_gradient)


def solution(mesh):
    return jax.shard_map(
        shards,
        mesh=mesh,
        in_specs=(
            P("seq", "chan"),
            P(None, None, None, "chan"),
            P(None, "chan"),
            P("seq", "chan"),
            P("seq", None),
        ),
        out_specs=(
            P("seq", "chan"),
            P("seq", "chan"),
            P("seq", "chan"),
            P(None, None, "seq", "chan"),
        ),
        check_vma=False,
    )
```

```python
import jax
import jax.numpy as jnp
from jax import lax
from jax.experimental import pallas as pl
from jax.experimental.pallas import tpu as pltpu
from jax.sharding import PartitionSpec as P

BLOCK = 128
EXONS = 8
NX, NY, NZ = 4, 4, 8
TAPS = 3
GROUP = 24
F32 = jnp.float32
BF = jnp.bfloat16


def activation_slope(point, cotan):
    _, back = jax.vjp(jax.nn.gelu, point)
    return back(cotan)[0]


def seq_index(y, z, core):
    return (y * NZ + z) * 2 + core


def shifted(value, steps):
    count = lax.axis_size("seq")
    leading, last = (max(0, -steps), min(count, count - steps))
    return lax.ppermute(value, "seq", [(s, s + steps) for s in range(leading, last)])


def along_x(value, steps):
    return lax.ppermute(value, "chan", [(i, (i + steps) % NX) for i in range(NX)])


def along_seq(value, dy, dz, dcore):
    pairs = [
        (
            seq_index(y, z, core),
            seq_index((y + dy) % NY, (z + dz) % NZ, (core + dcore) % 2),
        )
        for y in range(NY)
        for z in range(NZ)
        for core in range(2)
    ]
    return lax.ppermute(value, "seq", pairs)


def from_all_x(value):
    return [value] + [along_x(value, -r) for r in range(1, NX)]


def times_t(left, right):
    return lax.dot_general(left, right, (((1,), (1,)), ((), ())), preferred_element_type=F32)


def call(body, place, operands, outs, scratch=(), after=(), limit=16, flops=0, moved=0):
    count = len(operands)

    def kernel(*refs):
        body(refs[0], *refs[1 : 1 + count], *refs[1 + count + len(after) :])

    vmem = pl.BlockSpec(memory_space=pltpu.VMEM)
    return pl.pallas_call(
        kernel,
        in_specs=[pl.BlockSpec(memory_space=pltpu.SMEM)]
        + [pl.BlockSpec(memory_space=space) for _, space in operands]
        + [pl.BlockSpec(memory_space=pl.ANY)] * len(after),
        out_specs=[vmem] * len(outs),
        scratch_shapes=list(scratch),
        out_shape=outs,
        cost_estimate=pl.CostEstimate(flops=flops, bytes_accessed=moved, transcendentals=0),
        compiler_params=pltpu.CompilerParams(vmem_limit_bytes=limit * 2**20),
    )(place, *[value for value, _ in operands], *after)


def local(values):
    return [(value, pltpu.VMEM) for value in values]


def like(shape, dtype):
    return jax.ShapeDtypeStruct(shape, dtype)


def slot(place, r, width):
    return pl.ds(pl.multiple_of(lax.rem(place[0] + r, NX) * width, 128), width)


def conv_products(place, blocks, conv_weight, after):
    size, width = blocks[0].shape
    tall = NX * width

    def body(place, b0, b1, b2, b3, weight, low, mid, up, whole):
        for r, block in enumerate((b0, b1, b2, b3)):
            whole[:, slot(place, r, width)] = block[...]
        for k, ref in ((0, low), (2, up), (1, mid)):
            product = jnp.dot(whole[...], weight[0, k], preferred_element_type=F32)
            ref[...] = product.astype(ref.dtype)

    block = (size, width)
    return call(
        body,
        place,
        local(blocks + [conv_weight]),
        [like(block, BF), like(block, F32), like(block, BF), like((size, tall), BF)],
        after=after,
        flops=2 * size * tall * TAPS * width,
        moved=2 * tall * TAPS * width,
    )


def turned_blocks(place, whole, after):
    size, tall = whole.shape
    width = tall // NY

    def body(place, whole, *outs):
        for m, out in enumerate(outs):
            at = pl.multiple_of(lax.rem(place[1] + m, NY) * width, 128)
            out[...] = whole[:, pl.ds(at, width)].T

    return call(
        body,
        place,
        local([whole]),
        [like((width, size), BF)] * NY,
        after=after,
        flops=size * tall,
        moved=4 * size * tall,
    )


def stacked(place, values, after):
    shape = values[0].shape

    def body(place, *refs):
        for i in range(len(values)):
            refs[-1][i] = refs[i][...]

    return call(
        body,
        place,
        local(values),
        [like((len(values),) + shape, BF)],
        after=after,
        moved=4 * len(values) * values[0].size,
    )[0]


def token(value):
    return value[(0,) * (value.ndim - 2) + (slice(8), slice(128))]


def track_head(place, blocks, head_weight, head_cot, after):
    size, width = blocks[0].shape
    tall, wide = head_weight.shape
    tile = 256
    groups = size // BLOCK

    def body(place, b0, b1, b2, b3, weight, cot, out, sums, o0, o1, o2, o3, whole, term):
        for r, block in enumerate((b0, b1, b2, b3)):
            whole[:, slot(place, r, width)] = block[...]
        for j in range(wide // tile):
            cols = slice(j * tile, (j + 1) * tile)
            logits = jnp.dot(whole[...], weight[:, cols], preferred_element_type=F32)
            decay = jnp.exp(-jnp.abs(logits))
            above = 1.0 + decay
            log = jnp.where(decay < 1e-3, decay - 0.5 * decay * decay, jnp.log(above))
            track = (jnp.maximum(logits, 0.0) + log).astype(BF)
            out[:, cols] = track
            sums[:, cols] = jnp.sum(track.astype(F32).reshape(groups, BLOCK, tile), axis=1)
            part = pl.reciprocal(above, approx=True)
            part = part * (2.0 - above * part)
            sigmoid = jnp.where(logits >= 0.0, part, decay * part)
            term[:, cols] = (cot[:, cols].astype(F32) * sigmoid).astype(BF)
        for r, ref in ((2, o2), (1, o1), (3, o3), (0, o0)):
            ref[...] = times_t(term[...], weight[slot(place, r, width), :]).astype(ref.dtype)

    block = (size, width)
    return call(
        body,
        place,
        local(blocks + [head_weight, head_cot]),
        [like((size, wide), BF), like((groups, wide), F32), like(block, F32)] + [like(block, BF)] * 3,
        scratch=[pltpu.VMEM((size, tall), BF), pltpu.VMEM((size, wide), BF)],
        after=after,
        flops=4 * size * tall * wide,
        moved=2 * tall * wide,
    )


EXTRA = 16


def add_up(place, own, came, sums, after):
    size, width = own.shape
    groups, wide = sums.shape

    def body(place, own, c1, c2, c3, sums, total, low, long, below):
        value = own[...] + c1[...].astype(F32) + c2[...].astype(F32) + c3[...].astype(F32)
        total[...] = value
        low[...] = value.astype(BF)
        long[:size, :] = value.astype(BF)
        below[...] = jnp.zeros((EXTRA, width), F32)
        for i in range(TAPS):
            cols = min(width, wide - i * width)
            below[i * groups : (i + 1) * groups, :cols] = sums[:, i * width : i * width + cols]
        long[size:, :] = below[...].astype(BF)

    return call(
        body,
        place,
        local([own] + came + [sums]),
        [like((size, width), F32), like((size, width), BF), like((size + EXTRA, width), BF)],
        scratch=[pltpu.VMEM((EXTRA, width), F32)],
        after=after,
        flops=4 * own.size,
        moved=16 * own.size,
    )


def back_products(place, around, conv_weight, after):
    size, width = around[0].shape
    tall = NX * width
    cols = TAPS * width

    def body(place, d0, d1, d2, weight, o0, o1, o2, o3):
        for r, ref in ((2, o2), (1, o1), (3, o3), (0, o0)):
            at = slot(place, r, width)
            total = times_t(d0[...], weight[0, 0, at, :])
            total += times_t(d1[...], weight[0, 1, at, :])
            total += times_t(d2[...], weight[0, 2, at, :])
            ref[...] = total.astype(ref.dtype)

    block = (size, width)
    return call(
        body,
        place,
        local(around + [conv_weight]),
        [like(block, F32)] + [like(block, BF)] * 3,
        after=after,
        flops=2 * size * tall * cols,
        moved=2 * tall * cols,
    )


def kernel_terms(place, earlier, own, later, cots, after):
    _, width, size = own.shape
    half = width // 2
    cols = TAPS * width

    def body(place, earlier, own, later, d0, d1, d2, d3, kept, sent):
        y, z, core = place[1], place[2], place[3]
        first, last = z == 0, z == NZ - 1
        for k, left in enumerate((earlier, own, later)):
            total = jnp.zeros((width, width), F32)
            for m, right in enumerate((d0, d1, d2, d3)):
                if k == 0:
                    index = jnp.where(first, (m + 1) % NY, m)
                    valid = jnp.logical_not(jnp.logical_and(first, y == m))
                elif k == 2:
                    index = jnp.where(last, (m + NY - 1) % NY, m)
                    valid = jnp.logical_not(jnp.logical_and(last, y == (m + NY - 1) % NY))
                else:
                    index, valid = m, None
                product = jnp.dot(left[index], right[:size, :], preferred_element_type=F32)
                total += product if valid is None else jnp.where(valid, product, 0.0)
            pairs = total.reshape(half // GROUP, 2, GROUP, width)
            one, two = (pairs[:, i].reshape(half, width) for i in range(2))
            at = slice(k * width, (k + 1) * width)
            kept[:, at] = jnp.where(core == 0, one, two)
            sent[:, at] = jnp.where(core == 0, two, one).astype(BF)

    return call(
        body,
        place,
        local([earlier, own, later] + cots),
        [like((half, cols), F32), like((half, cols), BF)],
        after=after,
        flops=2 * size * NY * width * cols,
        moved=8 * NY * width * size,
    )


def over_z(place, kept, came, cover, after):
    rows, cols = kept.shape

    def body(place, kept, came, cover, *refs):
        outs, total, message = refs[:NZ], refs[NZ], refs[NZ + 1]
        total[...] = kept[...] + came[...].astype(F32)
        message[:EXTRA, :] = cover[...].astype(F32)
        for m, ref in enumerate(outs):
            at = pl.multiple_of(lax.rem(place[2] + m, NZ) * GROUP, 8)
            if m == 0:
                ref[...] = total[pl.ds(at, GROUP), :]
            else:
                message[EXTRA:, :] = total[pl.ds(at, GROUP), :]
                ref[...] = message[...].astype(BF)

    return call(
        body,
        place,
        local([kept, came, cover]),
        [like((GROUP, cols), F32)] + [like((EXTRA + GROUP, cols), BF)] * (NZ - 1),
        scratch=[pltpu.VMEM((rows, cols), F32), pltpu.VMEM((EXTRA + GROUP, cols), F32)],
        after=after,
        flops=4 * rows * cols,
        moved=6 * rows * cols,
    )


def coverage_of(blocks, place, exon_blocks, own):
    _, y, z, core = (place[i] for i in range(4))
    flip, dz, dy, part = jnp.meshgrid(
        *(jnp.arange(n, dtype=jnp.int32) for n in (2, NZ, NY, own)), indexing="ij"
    )
    labels = seq_index((y + NY - dy) % NY, (z + NZ - dz) % NZ, core ^ flip) * own + part
    labels = labels.reshape(-1)
    counts = (exon_blocks[:, :, None] == labels[None, None]).astype(F32).sum(axis=1)
    total = jnp.dot(
        counts.astype(BF), blocks.reshape(labels.shape[0], -1), preferred_element_type=F32
    )
    return total / jnp.sqrt(F32(EXONS * BLOCK))


def shards(inputs, conv_weight, head_weight, head_cot, exon_blocks):
    size, width = inputs.shape
    wide = head_cot.shape[1]
    own = size // BLOCK
    x = lax.axis_index("chan")
    s = lax.axis_index("seq")
    core, z, y = s % 2, (s // 2) % NZ, s // (2 * NZ)
    place = jnp.stack([x, y, z, core]).astype(jnp.int32)
    steps = 2

    state = inputs.astype(F32)
    acted = from_all_x(jax.nn.gelu(state).astype(BF))
    low, mid, up, whole = conv_products(place, acted, conv_weight, ())
    low, up = shifted(low, steps), shifted(up, -steps)
    after_conv = (state + (mid + low.astype(F32) + up.astype(F32))).astype(BF)
    full = from_all_x(after_conv)
    turned = turned_blocks(place, whole, (token(after_conv),))
    turned = [turned[0]] + [along_seq(turned[m], m, 0, 0) for m in range(1, NY)]
    turned = stacked(place, turned, tuple(token(value) for value in full[1:]))
    before = along_seq(turned, 0, 1, 0)
    behind = along_seq(turned, 0, NZ - 1, 0)

    tracks, sums, *blocks = track_head(place, full, head_weight, head_cot, (token(turned),))
    came = [along_x(blocks[r], r) for r in range(1, NX)]
    grad, low, long = add_up(place, blocks[0], came, sums, (token(before), token(behind)))
    cots = [long] + [along_seq(long, m, 0, 0) for m in range(1, NY)]
    around = [shifted(low, -steps), low, shifted(low, steps)]
    blocks = back_products(place, around, conv_weight, ())
    came = [along_x(blocks[r], r) for r in range(1, NX)]
    kept, sent = kernel_terms(place, before, turned, behind, cots, (token(blocks[1]),))
    cover = [
        cot[size : size + TAPS * own].reshape(TAPS, own, width).transpose(1, 0, 2).reshape(own, -1)
        for cot in cots
    ]
    cover = jnp.concatenate(cover, axis=0)
    kept, *parts = over_z(place, kept, along_seq(sent, 0, 0, 1), cover, ())
    parts = [along_seq(part, 0, m + 1, 0) for m, part in enumerate(parts)]
    for part in parts:
        kept = kept + part[EXTRA:].astype(F32)
    kernel_gradient = kept.reshape(GROUP, TAPS, width).transpose(1, 0, 2)[None]

    cover = jnp.stack([cover] + [part[:EXTRA] for part in parts])[:, :, :wide]
    cover = jnp.stack([cover, along_seq(cover, 0, 0, 1)])
    coverage = coverage_of(cover, place, exon_blocks, own)
    back_u = blocks[0] + came[0].astype(F32) + came[1].astype(F32) + came[2].astype(F32)
    out = (grad + activation_slope(state, back_u)).astype(BF)
    return (tracks, coverage, out, kernel_gradient)


def solution(mesh):
    return jax.shard_map(
        shards,
        mesh=mesh,
        in_specs=(
            P("seq", "chan"),
            P(None, None, None, "chan"),
            P(None, "chan"),
            P("seq", "chan"),
            P("seq", None),
        ),
        out_specs=(
            P("seq", "chan"),
            P("seq", "chan"),
            P("seq", "chan"),
            P(None, None, "seq", "chan"),
        ),
        check_vma=False,
    )
```

```python
import jax
import jax.numpy as jnp
from jax import lax
from jax.experimental import pallas as pl
from jax.experimental.pallas import tpu as pltpu
from jax.sharding import PartitionSpec as P

BLOCK = 128
EXONS = 8
NX, NY, NZ = 4, 4, 8
TAPS = 3
GROUP = 24
F32 = jnp.float32
BF = jnp.bfloat16


def activation_slope(point, cotan):
    _, back = jax.vjp(jax.nn.gelu, point)
    return back(cotan)[0]


def seq_index(y, z, core):
    return (y * NZ + z) * 2 + core


def shifted(value, steps):
    count = lax.axis_size("seq")
    leading, last = (max(0, -steps), min(count, count - steps))
    return lax.ppermute(value, "seq", [(s, s + steps) for s in range(leading, last)])


def along_x(value, steps):
    return lax.ppermute(value, "chan", [(i, (i + steps) % NX) for i in range(NX)])


def along_seq(value, dy, dz, dcore):
    pairs = [
        (
            seq_index(y, z, core),
            seq_index((y + dy) % NY, (z + dz) % NZ, (core + dcore) % 2),
        )
        for y in range(NY)
        for z in range(NZ)
        for core in range(2)
    ]
    return lax.ppermute(value, "seq", pairs)


def from_all_x(value):
    return [value] + [along_x(value, -r) for r in range(1, NX)]


def times_t(left, right):
    return lax.dot_general(left, right, (((1,), (1,)), ((), ())), preferred_element_type=F32)


def call(body, place, operands, outs, scratch=(), after=(), limit=16, flops=0, moved=0):
    count = len(operands)

    def kernel(*refs):
        body(refs[0], *refs[1 : 1 + count], *refs[1 + count + len(after) :])

    vmem = pl.BlockSpec(memory_space=pltpu.VMEM)
    return pl.pallas_call(
        kernel,
        in_specs=[pl.BlockSpec(memory_space=pltpu.SMEM)]
        + [pl.BlockSpec(memory_space=space) for _, space in operands]
        + [pl.BlockSpec(memory_space=pl.ANY)] * len(after),
        out_specs=[vmem] * len(outs),
        scratch_shapes=list(scratch),
        out_shape=outs,
        cost_estimate=pl.CostEstimate(flops=flops, bytes_accessed=moved, transcendentals=0),
        compiler_params=pltpu.CompilerParams(vmem_limit_bytes=limit * 2**20),
    )(place, *[value for value, _ in operands], *after)


def local(values):
    return [(value, pltpu.VMEM) for value in values]


def like(shape, dtype):
    return jax.ShapeDtypeStruct(shape, dtype)


def slot(place, r, width):
    return pl.ds(pl.multiple_of(lax.rem(place[0] + r, NX) * width, 128), width)


def conv_products(place, blocks, conv_weight, after):
    size, width = blocks[0].shape
    tall = NX * width

    def body(place, b0, b1, b2, b3, weight, low, mid, up, whole):
        for r, block in enumerate((b0, b1, b2, b3)):
            whole[:, slot(place, r, width)] = block[...]
        for k, ref in ((0, low), (2, up), (1, mid)):
            product = jnp.dot(whole[...], weight[0, k], preferred_element_type=F32)
            ref[...] = product.astype(ref.dtype)

    block = (size, width)
    return call(
        body,
        place,
        local(blocks + [conv_weight]),
        [like(block, BF), like(block, F32), like(block, BF), like((size, tall), BF)],
        after=after,
        flops=2 * size * tall * TAPS * width,
        moved=2 * tall * TAPS * width,
    )


def load(place, values, after):
    count = len(values)

    def body(place, *refs):
        sems = refs[-1]
        copies = [pltpu.make_async_copy(refs[i], refs[count + i], sems.at[i]) for i in range(count)]
        for copy in copies:
            copy.start()
        for copy in copies:
            copy.wait()

    return call(
        body,
        place,
        [(value, pl.ANY) for value in values],
        [like(value.shape, value.dtype) for value in values],
        scratch=[pltpu.SemaphoreType.DMA((count,))],
        after=after,
        moved=sum(4 * value.size for value in values),
    )


def turned_blocks(place, whole, after):
    size, tall = whole.shape
    width = tall // NY

    def body(place, whole, *outs):
        for m, out in enumerate(outs):
            at = pl.multiple_of(lax.rem(place[1] + m, NY) * width, 128)
            out[...] = whole[:, pl.ds(at, width)].T

    return call(
        body,
        place,
        local([whole]),
        [like((width, size), BF)] * NY,
        after=after,
        flops=size * tall,
        moved=4 * size * tall,
    )


def stacked(place, values, after):
    shape = values[0].shape

    def body(place, *refs):
        for i in range(len(values)):
            refs[-1][i] = refs[i][...]

    return call(
        body,
        place,
        local(values),
        [like((len(values),) + shape, BF)],
        after=after,
        moved=4 * len(values) * values[0].size,
    )[0]


def token(value):
    return value[(0,) * (value.ndim - 2) + (slice(8), slice(128))]


def track_head(place, blocks, head_weight, head_cot, after):
    size, width = blocks[0].shape
    tall, wide = head_weight.shape
    tile = 256
    groups = size // BLOCK

    def body(place, b0, b1, b2, b3, weight, cot, out, sums, o0, o1, o2, o3, whole, term):
        for r, block in enumerate((b0, b1, b2, b3)):
            whole[:, slot(place, r, width)] = block[...]
        for j in range(wide // tile):
            cols = slice(j * tile, (j + 1) * tile)
            logits = jnp.dot(whole[...], weight[:, cols], preferred_element_type=F32)
            decay = jnp.exp(-jnp.abs(logits))
            above = 1.0 + decay
            log = jnp.where(decay < 1e-3, decay - 0.5 * decay * decay, jnp.log(above))
            track = (jnp.maximum(logits, 0.0) + log).astype(BF)
            out[:, cols] = track
            sums[:, cols] = jnp.sum(track.astype(F32).reshape(groups, BLOCK, tile), axis=1)
            part = pl.reciprocal(above, approx=True)
            part = part * (2.0 - above * part)
            sigmoid = jnp.where(logits >= 0.0, part, decay * part)
            term[:, cols] = (cot[:, cols].astype(F32) * sigmoid).astype(BF)
        for r, ref in ((2, o2), (1, o1), (3, o3), (0, o0)):
            ref[...] = times_t(term[...], weight[slot(place, r, width), :]).astype(ref.dtype)

    block = (size, width)
    return call(
        body,
        place,
        local(blocks + [head_weight, head_cot]),
        [like((size, wide), BF), like((groups, wide), F32), like(block, F32)] + [like(block, BF)] * 3,
        scratch=[pltpu.VMEM((size, tall), BF), pltpu.VMEM((size, wide), BF)],
        after=after,
        flops=4 * size * tall * wide,
        moved=2 * tall * wide,
    )


EXTRA = 16


def add_up(place, own, came, sums, after):
    size, width = own.shape
    groups, wide = sums.shape

    def body(place, own, c1, c2, c3, sums, total, low, long, below):
        value = own[...] + c1[...].astype(F32) + c2[...].astype(F32) + c3[...].astype(F32)
        total[...] = value
        low[...] = value.astype(BF)
        long[:size, :] = value.astype(BF)
        below[...] = jnp.zeros((EXTRA, width), F32)
        for i in range(TAPS):
            cols = min(width, wide - i * width)
            below[i * groups : (i + 1) * groups, :cols] = sums[:, i * width : i * width + cols]
        long[size:, :] = below[...].astype(BF)

    return call(
        body,
        place,
        local([own] + came + [sums]),
        [like((size, width), F32), like((size, width), BF), like((size + EXTRA, width), BF)],
        scratch=[pltpu.VMEM((EXTRA, width), F32)],
        after=after,
        flops=4 * own.size,
        moved=16 * own.size,
    )


def back_products(place, around, conv_weight, after):
    size, width = around[0].shape
    tall = NX * width
    cols = TAPS * width

    def body(place, d0, d1, d2, weight, o0, o1, o2, o3):
        for r, ref in ((2, o2), (1, o1), (3, o3), (0, o0)):
            at = slot(place, r, width)
            total = times_t(d0[...], weight[0, 0, at, :])
            total += times_t(d1[...], weight[0, 1, at, :])
            total += times_t(d2[...], weight[0, 2, at, :])
            ref[...] = total.astype(ref.dtype)

    block = (size, width)
    return call(
        body,
        place,
        local(around + [conv_weight]),
        [like(block, F32)] + [like(block, BF)] * 3,
        after=after,
        flops=2 * size * tall * cols,
        moved=2 * tall * cols,
    )


def kernel_terms(place, earlier, own, later, cots, groups, after):
    _, width, size = own.shape
    half = width // 2
    cols = TAPS * width

    def body(place, earlier, own, later, d0, d1, d2, d3, kept, sent, cover, below):
        y, z, core = place[1], place[2], place[3]
        first, last = z == 0, z == NZ - 1
        for k, left in enumerate((earlier, own, later)):
            total = jnp.zeros((width, width), F32)
            for m, right in enumerate((d0, d1, d2, d3)):
                if k == 0:
                    index = jnp.where(first, (m + 1) % NY, m)
                    valid = jnp.logical_not(jnp.logical_and(first, y == m))
                elif k == 2:
                    index = jnp.where(last, (m + NY - 1) % NY, m)
                    valid = jnp.logical_not(jnp.logical_and(last, y == (m + NY - 1) % NY))
                else:
                    index, valid = m, None
                product = jnp.dot(left[index], right[:size, :], preferred_element_type=F32)
                total += product if valid is None else jnp.where(valid, product, 0.0)
            pairs = total.reshape(half // GROUP, 2, GROUP, width)
            one, two = (pairs[:, i].reshape(half, width) for i in range(2))
            at = slice(k * width, (k + 1) * width)
            kept[:, at] = jnp.where(core == 0, one, two)
            sent[:, at] = jnp.where(core == 0, two, one).astype(BF)
        for m, right in enumerate((d0, d1, d2, d3)):
            below[...] = right[size:, :].astype(F32)
            for i in range(TAPS):
                cover[m * groups : (m + 1) * groups, i * width : (i + 1) * width] = below[
                    i * groups : (i + 1) * groups, :
                ]

    return call(
        body,
        place,
        local([earlier, own, later] + cots),
        [like((half, cols), F32), like((half, cols), BF), like((NY * groups, cols), F32)],
        scratch=[pltpu.VMEM((EXTRA, width), F32)],
        after=after,
        flops=2 * size * NY * width * cols,
        moved=8 * NY * width * size,
    )


def over_z(place, kept, came, cover, after):
    rows, cols = kept.shape

    def body(place, kept, came, cover, *refs):
        outs, total, message = refs[:NZ], refs[NZ], refs[NZ + 1]
        total[...] = kept[...] + came[...].astype(F32)
        message[:EXTRA, :] = cover[...]
        for m, ref in enumerate(outs):
            at = pl.multiple_of(lax.rem(place[2] + m, NZ) * GROUP, 8)
            if m == 0:
                ref[...] = total[pl.ds(at, GROUP), :]
            else:
                message[EXTRA:, :] = total[pl.ds(at, GROUP), :]
                ref[...] = message[...].astype(BF)

    return call(
        body,
        place,
        local([kept, came, cover]),
        [like((GROUP, cols), F32)] + [like((EXTRA + GROUP, cols), BF)] * (NZ - 1),
        scratch=[pltpu.VMEM((rows, cols), F32), pltpu.VMEM((EXTRA + GROUP, cols), F32)],
        after=after,
        flops=4 * rows * cols,
        moved=6 * rows * cols,
    )


def input_gradient(place, inputs, grad, own, came, after):
    def body(place, state, grad, own, c1, c2, c3, out):
        back_u = own[...] + c1[...].astype(F32) + c2[...].astype(F32) + c3[...].astype(F32)
        out[...] = (grad[...] + activation_slope(state[...].astype(F32), back_u)).astype(BF)

    return call(
        body,
        place,
        local([inputs, grad, own] + came),
        [like(inputs.shape, BF)],
        after=after,
        flops=20 * inputs.size,
        moved=16 * inputs.size,
    )[0]


def coverage_of(blocks, place, exon_blocks, own):
    _, y, z, core = (place[i] for i in range(4))
    flip, dz, dy, part = jnp.meshgrid(
        *(jnp.arange(n, dtype=jnp.int32) for n in (2, NZ, NY, own)), indexing="ij"
    )
    labels = seq_index((y + NY - dy) % NY, (z + NZ - dz) % NZ, core ^ flip) * own + part
    labels = labels.reshape(-1)
    counts = (exon_blocks[:, :, None] == labels[None, None]).astype(F32).sum(axis=1)
    total = jnp.dot(
        counts.astype(BF), blocks.reshape(labels.shape[0], -1), preferred_element_type=F32
    )
    return total / jnp.sqrt(F32(EXONS * BLOCK))


def shards(inputs, conv_weight, head_weight, head_cot, exon_blocks):
    size, width = inputs.shape
    wide = head_cot.shape[1]
    own = size // BLOCK
    x = lax.axis_index("chan")
    s = lax.axis_index("seq")
    core, z, y = s % 2, (s // 2) % NZ, s // (2 * NZ)
    place = jnp.stack([x, y, z, core]).astype(jnp.int32)
    steps = 2

    state = inputs.astype(F32)
    acted = from_all_x(jax.nn.gelu(state).astype(BF))
    (taps,) = load(place, [conv_weight], (token(acted[0]),))
    low, mid, up, whole = conv_products(place, acted, taps, ())
    low, up = shifted(low, steps), shifted(up, -steps)
    after_conv = (state + (mid + low.astype(F32) + up.astype(F32))).astype(BF)
    full = from_all_x(after_conv)
    turned = turned_blocks(place, whole, (token(after_conv),))
    turned = [turned[0]] + [along_seq(turned[m], m, 0, 0) for m in range(1, NY)]

    head, cot = load(place, [head_weight, head_cot], (token(after_conv),))
    turned = stacked(place, turned, tuple(token(value) for value in full[1:]))
    before = along_seq(turned, 0, 1, 0)
    behind = along_seq(turned, 0, NZ - 1, 0)
    tracks, sums, *blocks = track_head(place, full, head, cot, (token(turned),))
    came = [along_x(blocks[r], r) for r in range(1, NX)]
    (taps,) = load(place, [conv_weight], (token(blocks[1]),))
    grad, low, long = add_up(place, blocks[0], came, sums, (token(before), token(behind)))

    cots = [long] + [along_seq(long, m, 0, 0) for m in range(1, NY)]
    around = [shifted(low, -steps), low, shifted(low, steps)]
    blocks = back_products(place, around, taps, ())
    came = [along_x(blocks[r], r) for r in range(1, NX)]
    kept, sent, cover = kernel_terms(place, before, turned, behind, cots, own, (token(blocks[1]),))
    kept, *parts = over_z(place, kept, along_seq(sent, 0, 0, 1), cover, tuple(token(value) for value in came))
    out = input_gradient(place, inputs, grad, blocks[0], came, (token(parts[-1]),))
    parts = [along_seq(part, 0, m + 1, 0) for m, part in enumerate(parts)]
    for part in parts:
        kept = kept + part[EXTRA:].astype(F32)
    kernel_gradient = kept.reshape(GROUP, TAPS, width).transpose(1, 0, 2)[None]

    cover = jnp.stack([cover.astype(BF)] + [part[:EXTRA] for part in parts])[:, :, :wide]
    cover = jnp.stack([cover, along_seq(cover, 0, 0, 1)])
    coverage = coverage_of(cover, place, exon_blocks, own)
    return (tracks, coverage, out, kernel_gradient)


def solution(mesh):
    return jax.shard_map(
        shards,
        mesh=mesh,
        in_specs=(
            P("seq", "chan"),
            P(None, None, None, "chan"),
            P(None, "chan"),
            P("seq", "chan"),
            P("seq", None),
        ),
        out_specs=(
            P("seq", "chan"),
            P("seq", "chan"),
            P("seq", "chan"),
            P(None, None, "seq", "chan"),
        ),
        check_vma=False,
    )
```

```python
import jax
import jax.numpy as jnp
from jax import lax
from jax.experimental import pallas as pl
from jax.experimental.pallas import tpu as pltpu
from jax.sharding import PartitionSpec as P

BLOCK = 128
EXONS = 8
NX, NY, NZ = 4, 4, 8
TAPS = 3
GROUP = 24
F32 = jnp.float32
BF = jnp.bfloat16


def activation_slope(point, cotan):
    _, back = jax.vjp(jax.nn.gelu, point)
    return back(cotan)[0]


def seq_index(y, z, core):
    return (y * NZ + z) * 2 + core


def shifted(value, steps):
    count = lax.axis_size("seq")
    leading, last = (max(0, -steps), min(count, count - steps))
    return lax.ppermute(value, "seq", [(s, s + steps) for s in range(leading, last)])


def along_x(value, steps):
    return lax.ppermute(value, "chan", [(i, (i + steps) % NX) for i in range(NX)])


def along_seq(value, dy, dz, dcore):
    pairs = [
        (
            seq_index(y, z, core),
            seq_index((y + dy) % NY, (z + dz) % NZ, (core + dcore) % 2),
        )
        for y in range(NY)
        for z in range(NZ)
        for core in range(2)
    ]
    return lax.ppermute(value, "seq", pairs)


def from_all_x(value):
    return [value] + [along_x(value, -r) for r in range(1, NX)]


def times_t(left, right):
    return lax.dot_general(left, right, (((1,), (1,)), ((), ())), preferred_element_type=F32)


def call(body, place, operands, outs, scratch=(), after=(), limit=16, flops=0, moved=0):
    count = len(operands)

    def kernel(*refs):
        body(refs[0], *refs[1 : 1 + count], *refs[1 + count + len(after) :])

    vmem = pl.BlockSpec(memory_space=pltpu.VMEM)
    return pl.pallas_call(
        kernel,
        in_specs=[pl.BlockSpec(memory_space=pltpu.SMEM)]
        + [pl.BlockSpec(memory_space=space) for _, space in operands]
        + [pl.BlockSpec(memory_space=pl.ANY)] * len(after),
        out_specs=[vmem] * len(outs),
        scratch_shapes=list(scratch),
        out_shape=outs,
        cost_estimate=pl.CostEstimate(flops=flops, bytes_accessed=moved, transcendentals=0),
        compiler_params=pltpu.CompilerParams(vmem_limit_bytes=limit * 2**20),
    )(place, *[value for value, _ in operands], *after)


def local(values):
    return [(value, pltpu.VMEM) for value in values]


def like(shape, dtype):
    return jax.ShapeDtypeStruct(shape, dtype)


def slot(place, r, width):
    return pl.ds(pl.multiple_of(lax.rem(place[0] + r, NX) * width, 128), width)


def conv_products(place, blocks, conv_weight, after):
    size, width = blocks[0].shape
    tall = NX * width

    def body(place, b0, b1, b2, b3, weight, low, mid, up, whole):
        for r, block in enumerate((b0, b1, b2, b3)):
            whole[:, slot(place, r, width)] = block[...]
        for k, ref in ((0, low), (2, up), (1, mid)):
            product = jnp.dot(whole[...], weight[0, k], preferred_element_type=F32)
            ref[...] = product.astype(ref.dtype)

    block = (size, width)
    return call(
        body,
        place,
        local(blocks + [conv_weight]),
        [like(block, BF), like(block, F32), like(block, BF), like((size, tall), BF)],
        after=after,
        flops=2 * size * tall * TAPS * width,
        moved=2 * tall * TAPS * width,
    )


def load(place, values, after):
    count = len(values)

    def body(place, *refs):
        sems = refs[-1]
        copies = [pltpu.make_async_copy(refs[i], refs[count + i], sems.at[i]) for i in range(count)]
        for copy in copies:
            copy.start()
        for copy in copies:
            copy.wait()

    return call(
        body,
        place,
        [(value, pl.ANY) for value in values],
        [like(value.shape, value.dtype) for value in values],
        scratch=[pltpu.SemaphoreType.DMA((count,))],
        after=after,
        moved=sum(4 * value.size for value in values),
    )


def turned_blocks(place, whole, after):
    size, tall = whole.shape
    width = tall // NY

    def body(place, whole, *outs):
        for m, out in enumerate(outs):
            at = pl.multiple_of(lax.rem(place[1] + m, NY) * width, 128)
            out[...] = whole[:, pl.ds(at, width)].T

    return call(
        body,
        place,
        local([whole]),
        [like((width, size), BF)] * NY,
        after=after,
        flops=size * tall,
        moved=4 * size * tall,
    )


def stacked(place, values, after):
    shape = values[0].shape

    def body(place, *refs):
        for i in range(len(values)):
            refs[-1][i] = refs[i][...]

    return call(
        body,
        place,
        local(values),
        [like((len(values),) + shape, BF)],
        after=after,
        moved=4 * len(values) * values[0].size,
    )[0]


def token(value):
    return value[(0,) * (value.ndim - 2) + (slice(8), slice(128))]


def track_head(place, blocks, head_weight, head_cot, after):
    size, width = blocks[0].shape
    tall, wide = head_weight.shape
    tile = 256
    groups = size // BLOCK

    def body(place, b0, b1, b2, b3, weight, cot, out, sums, o0, o1, o2, o3, done, whole, term):
        for r, block in enumerate((b0, b1, b2, b3)):
            whole[:, slot(place, r, width)] = block[...]
        for j in range(wide // tile):
            cols = slice(j * tile, (j + 1) * tile)
            logits = jnp.dot(whole[...], weight[:, cols], preferred_element_type=F32)
            decay = jnp.exp(-jnp.abs(logits))
            above = 1.0 + decay
            log = jnp.where(decay < 1e-3, decay - 0.5 * decay * decay, jnp.log(above))
            track = (jnp.maximum(logits, 0.0) + log).astype(BF)
            out[:, cols] = track
            sums[:, cols] = jnp.sum(track.astype(F32).reshape(groups, BLOCK, tile), axis=1)
            part = pl.reciprocal(above, approx=True)
            part = part * (2.0 - above * part)
            sigmoid = jnp.where(logits >= 0.0, part, decay * part)
            term[:, cols] = (cot[:, cols].astype(F32) * sigmoid).astype(BF)
        for r, ref in ((2, o2), (1, o1), (3, o3), (0, o0)):
            ref[...] = times_t(term[...], weight[slot(place, r, width), :]).astype(ref.dtype)
        done[...] = jnp.zeros_like(done)

    block = (size, width)
    return call(
        body,
        place,
        local(blocks + [head_weight, head_cot]),
        [like((size, wide), BF), like((groups, wide), F32), like(block, F32)] + [like(block, BF)] * 3 + [like((8, 128), F32)],
        scratch=[pltpu.VMEM((size, tall), BF), pltpu.VMEM((size, wide), BF)],
        after=after,
        flops=4 * size * tall * wide,
        moved=2 * tall * wide,
    )


EXTRA = 16


def add_up(place, own, came, sums, after):
    size, width = own.shape
    groups, wide = sums.shape

    def body(place, own, c1, c2, c3, sums, total, long, below):
        value = own[...] + c1[...].astype(F32) + c2[...].astype(F32) + c3[...].astype(F32)
        total[...] = value
        long[:size, :] = value.astype(BF)
        below[...] = jnp.zeros((EXTRA, width), F32)
        for i in range(TAPS):
            cols = min(width, wide - i * width)
            below[i * groups : (i + 1) * groups, :cols] = sums[:, i * width : i * width + cols]
        long[size:, :] = below[...].astype(BF)

    return call(
        body,
        place,
        local([own] + came + [sums]),
        [like((size, width), F32), like((size + EXTRA, width), BF)],
        scratch=[pltpu.VMEM((EXTRA, width), F32)],
        after=after,
        flops=4 * own.size,
        moved=16 * own.size,
    )


def rounded(place, value, after):
    def body(place, value, out):
        out[...] = value[...].astype(BF)

    return call(
        body,
        place,
        local([value]),
        [like(value.shape, BF)],
        after=after,
        flops=value.size,
        moved=200 * value.size,
    )[0]


def back_products(place, around, conv_weight, after):
    size, width = around[0].shape
    tall = NX * width
    cols = TAPS * width

    def body(place, d0, d1, d2, weight, o0, o1, o2, o3, done):
        for r, ref in ((2, o2), (1, o1), (3, o3), (0, o0)):
            at = slot(place, r, width)
            total = times_t(d0[...], weight[0, 0, at, :])
            total += times_t(d1[...], weight[0, 1, at, :])
            total += times_t(d2[...], weight[0, 2, at, :])
            ref[...] = total.astype(ref.dtype)
        done[...] = jnp.zeros_like(done)

    block = (size, width)
    return call(
        body,
        place,
        local(around + [conv_weight]),
        [like(block, F32)] + [like(block, BF)] * 3 + [like((8, 128), F32)],
        after=after,
        flops=2 * size * tall * cols,
        moved=2 * tall * cols,
    )


def kernel_terms(place, earlier, own, later, cots, groups, after):
    _, width, size = own.shape
    half = width // 2
    cols = TAPS * width

    def body(place, earlier, own, later, d0, d1, d2, d3, kept, sent, cover, below):
        y, z, core = place[1], place[2], place[3]
        first, last = z == 0, z == NZ - 1
        for k, left in enumerate((earlier, own, later)):
            total = jnp.zeros((width, width), F32)
            for m, right in enumerate((d0, d1, d2, d3)):
                if k == 0:
                    index = jnp.where(first, (m + 1) % NY, m)
                    valid = jnp.logical_not(jnp.logical_and(first, y == m))
                elif k == 2:
                    index = jnp.where(last, (m + NY - 1) % NY, m)
                    valid = jnp.logical_not(jnp.logical_and(last, y == (m + NY - 1) % NY))
                else:
                    index, valid = m, None
                product = jnp.dot(left[index], right[:size, :], preferred_element_type=F32)
                total += product if valid is None else jnp.where(valid, product, 0.0)
            pairs = total.reshape(half // GROUP, 2, GROUP, width)
            one, two = (pairs[:, i].reshape(half, width) for i in range(2))
            at = slice(k * width, (k + 1) * width)
            kept[:, at] = jnp.where(core == 0, one, two)
            sent[:, at] = jnp.where(core == 0, two, one).astype(BF)
        for m, right in enumerate((d0, d1, d2, d3)):
            below[...] = right[size:, :].astype(F32)
            for i in range(TAPS):
                cover[m * groups : (m + 1) * groups, i * width : (i + 1) * width] = below[
                    i * groups : (i + 1) * groups, :
                ]

    return call(
        body,
        place,
        local([earlier, own, later] + cots),
        [like((half, cols), F32), like((half, cols), BF), like((NY * groups, cols), F32)],
        scratch=[pltpu.VMEM((EXTRA, width), F32)],
        after=after,
        flops=2 * size * NY * width * cols,
        moved=8 * NY * width * size,
    )


def over_z(place, kept, came, cover, after):
    rows, cols = kept.shape

    def body(place, kept, came, cover, *refs):
        outs, total, message = refs[:NZ], refs[NZ], refs[NZ + 1]
        total[...] = kept[...] + came[...].astype(F32)
        message[:EXTRA, :] = cover[...]
        for m, ref in enumerate(outs):
            at = pl.multiple_of(lax.rem(place[2] + m, NZ) * GROUP, 8)
            if m == 0:
                ref[...] = total[pl.ds(at, GROUP), :]
            else:
                message[EXTRA:, :] = total[pl.ds(at, GROUP), :]
                ref[...] = message[...].astype(BF)

    return call(
        body,
        place,
        local([kept, came, cover]),
        [like((GROUP, cols), F32)] + [like((EXTRA + GROUP, cols), BF)] * (NZ - 1),
        scratch=[pltpu.VMEM((rows, cols), F32), pltpu.VMEM((EXTRA + GROUP, cols), F32)],
        after=after,
        flops=4 * rows * cols,
        moved=6 * rows * cols,
    )


def input_gradient(place, inputs, grad, own, came, after):
    def body(place, state, grad, own, c1, c2, c3, out, done):
        back_u = own[...] + c1[...].astype(F32) + c2[...].astype(F32) + c3[...].astype(F32)
        out[...] = (grad[...] + activation_slope(state[...].astype(F32), back_u)).astype(BF)
        done[...] = jnp.zeros_like(done)

    return call(
        body,
        place,
        local([inputs, grad, own] + came),
        [like(inputs.shape, BF), like((8, 128), F32)],
        after=after,
        flops=20 * inputs.size,
        moved=16 * inputs.size,
    )


def coverage_of(blocks, place, exon_blocks, own):
    _, y, z, core = (place[i] for i in range(4))
    flip, dz, dy, part = jnp.meshgrid(
        *(jnp.arange(n, dtype=jnp.int32) for n in (2, NZ, NY, own)), indexing="ij"
    )
    labels = seq_index((y + NY - dy) % NY, (z + NZ - dz) % NZ, core ^ flip) * own + part
    labels = labels.reshape(-1)
    counts = (exon_blocks[:, :, None] == labels[None, None]).astype(F32).sum(axis=1)
    total = jnp.dot(
        counts.astype(BF), blocks.reshape(labels.shape[0], -1), preferred_element_type=F32
    )
    return total / jnp.sqrt(F32(EXONS * BLOCK))


def shards(inputs, conv_weight, head_weight, head_cot, exon_blocks):
    size, width = inputs.shape
    wide = head_cot.shape[1]
    own = size // BLOCK
    x = lax.axis_index("chan")
    s = lax.axis_index("seq")
    core, z, y = s % 2, (s // 2) % NZ, s // (2 * NZ)
    place = jnp.stack([x, y, z, core]).astype(jnp.int32)
    steps = 2

    state = inputs.astype(F32)
    acted = from_all_x(jax.nn.gelu(state).astype(BF))
    (taps,) = load(place, [conv_weight], (token(acted[0]),))
    low, mid, up, whole = conv_products(place, acted, taps, ())
    low, up = shifted(low, steps), shifted(up, -steps)
    after_conv = (state + (mid + low.astype(F32) + up.astype(F32))).astype(BF)
    full = from_all_x(after_conv)
    turned = turned_blocks(place, whole, (token(after_conv),))
    turned = [turned[0]] + [along_seq(turned[m], m, 0, 0) for m in range(1, NY)]

    head, cot = load(place, [head_weight, head_cot], (token(after_conv),))
    tracks, sums, *blocks, done = track_head(place, full, head, cot, ())
    turned = stacked(place, turned, (done,))
    before = along_seq(turned, 0, 1, 0)
    behind = along_seq(turned, 0, NZ - 1, 0)
    came = [along_x(blocks[r], r) for r in range(1, NX)]
    (taps,) = load(place, [conv_weight], (done,))
    grad, long = add_up(place, blocks[0], came, sums, ())

    low = rounded(place, grad, (token(long),))
    cots = [long] + [along_seq(long, m, 0, 0) for m in range(1, NY)]
    around = [shifted(low, -steps), low, shifted(low, steps)]
    *blocks, done = back_products(place, around, taps, (token(before), token(behind)))
    came = [along_x(blocks[r], r) for r in range(1, NX)]
    kept, sent, cover = kernel_terms(place, before, turned, behind, cots, own, (done,))
    out, done = input_gradient(place, inputs, grad, blocks[0], came, ())
    kept, *parts = over_z(place, kept, along_seq(sent, 0, 0, 1), cover, (done,))
    parts = [along_seq(part, 0, m + 1, 0) for m, part in enumerate(parts)]
    for part in parts:
        kept = kept + part[EXTRA:].astype(F32)
    kernel_gradient = kept.reshape(GROUP, TAPS, width).transpose(1, 0, 2)[None]

    cover = jnp.stack([cover.astype(BF)] + [part[:EXTRA] for part in parts])[:, :, :wide]
    cover = jnp.stack([cover, along_seq(cover, 0, 0, 1)])
    coverage = coverage_of(cover, place, exon_blocks, own)
    return (tracks, coverage, out, kernel_gradient)


def solution(mesh):
    return jax.shard_map(
        shards,
        mesh=mesh,
        in_specs=(
            P("seq", "chan"),
            P(None, None, None, "chan"),
            P(None, "chan"),
            P("seq", "chan"),
            P("seq", None),
        ),
        out_specs=(
            P("seq", "chan"),
            P("seq", "chan"),
            P("seq", "chan"),
            P(None, None, "seq", "chan"),
        ),
        check_vma=False,
    )
```

```python
import jax
import jax.numpy as jnp
from jax import lax
from jax.experimental import pallas as pl
from jax.experimental.pallas import tpu as pltpu
from jax.sharding import PartitionSpec as P

BLOCK = 128
EXONS = 8
NX, NY, NZ = 4, 4, 8
TAPS = 3
GROUP = 24
F32 = jnp.float32
BF = jnp.bfloat16


def activation_slope(point, cotan):
    _, back = jax.vjp(jax.nn.gelu, point)
    return back(cotan)[0]


def seq_index(y, z, core):
    return (y * NZ + z) * 2 + core


def shifted(value, steps):
    count = lax.axis_size("seq")
    leading, last = (max(0, -steps), min(count, count - steps))
    return lax.ppermute(value, "seq", [(s, s + steps) for s in range(leading, last)])


def along_x(value, steps):
    return lax.ppermute(value, "chan", [(i, (i + steps) % NX) for i in range(NX)])


def along_seq(value, dy, dz, dcore):
    pairs = [
        (
            seq_index(y, z, core),
            seq_index((y + dy) % NY, (z + dz) % NZ, (core + dcore) % 2),
        )
        for y in range(NY)
        for z in range(NZ)
        for core in range(2)
    ]
    return lax.ppermute(value, "seq", pairs)


def from_all_x(value):
    return [value] + [along_x(value, -r) for r in range(1, NX)]


def times_t(left, right):
    return lax.dot_general(left, right, (((1,), (1,)), ((), ())), preferred_element_type=F32)


def call(body, place, operands, outs, scratch=(), after=(), limit=16, flops=0, moved=0):
    count = len(operands)

    def kernel(*refs):
        body(refs[0], *refs[1 : 1 + count], *refs[1 + count + len(after) :])

    vmem = pl.BlockSpec(memory_space=pltpu.VMEM)
    return pl.pallas_call(
        kernel,
        in_specs=[pl.BlockSpec(memory_space=pltpu.SMEM)]
        + [pl.BlockSpec(memory_space=space) for _, space in operands]
        + [pl.BlockSpec(memory_space=pl.ANY)] * len(after),
        out_specs=[vmem] * len(outs),
        scratch_shapes=list(scratch),
        out_shape=outs,
        cost_estimate=pl.CostEstimate(flops=flops, bytes_accessed=moved, transcendentals=0),
        compiler_params=pltpu.CompilerParams(vmem_limit_bytes=limit * 2**20),
    )(place, *[value for value, _ in operands], *after)


def local(values):
    return [(value, pltpu.VMEM) for value in values]


def like(shape, dtype):
    return jax.ShapeDtypeStruct(shape, dtype)


def slot(place, r, width):
    return pl.ds(pl.multiple_of(lax.rem(place[0] + r, NX) * width, 128), width)


def conv_products(place, blocks, conv_weight, after):
    size, width = blocks[0].shape
    tall = NX * width

    def body(place, b0, b1, b2, b3, weight, low, mid, up, whole):
        for r, block in enumerate((b0, b1, b2, b3)):
            whole[:, slot(place, r, width)] = block[...]
        for k, ref in ((0, low), (2, up), (1, mid)):
            product = jnp.dot(whole[...], weight[0, k], preferred_element_type=F32)
            ref[...] = product.astype(ref.dtype)

    block = (size, width)
    return call(
        body,
        place,
        local(blocks + [conv_weight]),
        [like(block, BF), like(block, F32), like(block, BF), like((size, tall), BF)],
        after=after,
        flops=2 * size * tall * TAPS * width,
        moved=2 * tall * TAPS * width,
    )


def load(place, values, after):
    count = len(values)

    def body(place, *refs):
        sems = refs[-1]
        copies = [pltpu.make_async_copy(refs[i], refs[count + i], sems.at[i]) for i in range(count)]
        for copy in copies:
            copy.start()
        for copy in copies:
            copy.wait()

    return call(
        body,
        place,
        [(value, pl.ANY) for value in values],
        [like(value.shape, value.dtype) for value in values],
        scratch=[pltpu.SemaphoreType.DMA((count,))],
        after=after,
        moved=sum(4 * value.size for value in values),
    )


def turned_blocks(place, whole, after):
    size, tall = whole.shape
    width = tall // NY

    def body(place, whole, *outs):
        for m, out in enumerate(outs):
            at = pl.multiple_of(lax.rem(place[1] + m, NY) * width, 128)
            out[...] = whole[:, pl.ds(at, width)].T

    return call(
        body,
        place,
        local([whole]),
        [like((width, size), BF)] * NY,
        after=after,
        flops=size * tall,
        moved=4 * size * tall,
    )


def stacked(place, values, after):
    rows, cols = values[0].shape

    def body(place, *refs):
        for i in range(len(values)):
            refs[-1][:, i * cols : (i + 1) * cols] = refs[i][...]

    return call(
        body,
        place,
        local(values),
        [like((rows, len(values) * cols), BF)],
        after=after,
        moved=4 * len(values) * values[0].size,
    )[0]


def token(value):
    return value[(0,) * (value.ndim - 2) + (slice(8), slice(128))]


def track_head(place, blocks, head_weight, head_cot, after):
    size, width = blocks[0].shape
    tall, wide = head_weight.shape
    tile = 256
    groups = size // BLOCK

    def body(place, b0, b1, b2, b3, weight, cot, out, sums, o0, o1, o2, o3, done, whole, term):
        for r, block in enumerate((b0, b1, b2, b3)):
            whole[:, slot(place, r, width)] = block[...]
        for j in range(wide // tile):
            cols = slice(j * tile, (j + 1) * tile)
            logits = jnp.dot(whole[...], weight[:, cols], preferred_element_type=F32)
            decay = jnp.exp(-jnp.abs(logits))
            above = 1.0 + decay
            log = jnp.where(decay < 1e-3, decay - 0.5 * decay * decay, jnp.log(above))
            track = (jnp.maximum(logits, 0.0) + log).astype(BF)
            out[:, cols] = track
            sums[:, cols] = jnp.sum(track.astype(F32).reshape(groups, BLOCK, tile), axis=1)
            part = pl.reciprocal(above, approx=True)
            part = part * (2.0 - above * part)
            sigmoid = jnp.where(logits >= 0.0, part, decay * part)
            term[:, cols] = (cot[:, cols].astype(F32) * sigmoid).astype(BF)
        for r, ref in ((2, o2), (1, o1), (3, o3), (0, o0)):
            ref[...] = times_t(term[...], weight[slot(place, r, width), :]).astype(ref.dtype)
        done[...] = jnp.zeros_like(done)

    block = (size, width)
    return call(
        body,
        place,
        local(blocks + [head_weight, head_cot]),
        [like((size, wide), BF), like((groups, wide), F32), like(block, F32)] + [like(block, BF)] * 3 + [like((8, 128), F32)],
        scratch=[pltpu.VMEM((size, tall), BF), pltpu.VMEM((size, wide), BF)],
        after=after,
        flops=4 * size * tall * wide,
        moved=2 * tall * wide,
    )


EXTRA = 16


def add_up(place, own, came, sums, after):
    size, width = own.shape
    groups, wide = sums.shape

    def body(place, own, c1, c2, c3, sums, total, low, long, below):
        value = own[...] + c1[...].astype(F32) + c2[...].astype(F32) + c3[...].astype(F32)
        total[...] = value
        low[...] = value.astype(BF)
        long[:size, :] = value.astype(BF)
        below[...] = jnp.zeros((EXTRA, width), F32)
        for i in range(TAPS):
            cols = min(width, wide - i * width)
            below[i * groups : (i + 1) * groups, :cols] = sums[:, i * width : i * width + cols]
        long[size:, :] = below[...].astype(BF)

    return call(
        body,
        place,
        local([own] + came + [sums]),
        [like((size, width), F32), like((size, width), BF), like((size + EXTRA, width), BF)],
        scratch=[pltpu.VMEM((EXTRA, width), F32)],
        after=after,
        flops=4 * own.size,
        moved=16 * own.size,
    )


def back_products(place, around, conv_weight, after):
    size, width = around[0].shape
    tall = NX * width
    cols = TAPS * width

    def body(place, d0, d1, d2, weight, o0, o1, o2, o3, done):
        for r, ref in ((2, o2), (1, o1), (3, o3), (0, o0)):
            at = slot(place, r, width)
            total = times_t(d0[...], weight[0, 0, at, :])
            total += times_t(d1[...], weight[0, 1, at, :])
            total += times_t(d2[...], weight[0, 2, at, :])
            ref[...] = total.astype(ref.dtype)
        done[...] = jnp.zeros_like(done)

    block = (size, width)
    return call(
        body,
        place,
        local(around + [conv_weight]),
        [like(block, F32)] + [like(block, BF)] * 3 + [like((8, 128), F32)],
        after=after,
        flops=2 * size * tall * cols,
        moved=2 * tall * cols,
    )


def kernel_terms(place, earlier, own, later, cots, groups, after):
    width, size = own.shape[0], own.shape[1] // NY
    half = width // 2
    cols = TAPS * width

    def body(place, earlier, own, later, d0, d1, d2, d3, kept, sent, cover, done, below, joined):
        y, z, core = place[1], place[2], place[3]
        first, last = z == 0, z == NZ - 1
        done[...] = jnp.zeros_like(done)
        for k, left in enumerate((earlier, own, later)):
            for m, right in enumerate((d0, d1, d2, d3)):
                if k == 0:
                    index = jnp.where(first, (m + 1) % NY, m)
                    valid = jnp.logical_not(jnp.logical_and(first, y == m))
                elif k == 2:
                    index = jnp.where(last, (m + NY - 1) % NY, m)
                    valid = jnp.logical_not(jnp.logical_and(last, y == (m + NY - 1) % NY))
                else:
                    joined[k, m * size : (m + 1) * size, :] = right[:size, :]
                    continue
                at = pl.ds(pl.multiple_of(index * size, size), size)

                @pl.when(valid)
                def _():
                    joined[k, at, :] = right[:size, :]

                @pl.when(jnp.logical_not(valid))
                def _():
                    joined[k, at, :] = jnp.zeros((size, width), BF)

        for k, left in enumerate((earlier, own, later)):
            total = jnp.dot(left[...], joined[k], preferred_element_type=F32)
            pairs = total.reshape(half // GROUP, 2, GROUP, width)
            one, two = (pairs[:, i].reshape(half, width) for i in range(2))
            at = slice(k * width, (k + 1) * width)
            kept[:, at] = jnp.where(core == 0, one, two)
            sent[:, at] = jnp.where(core == 0, two, one).astype(BF)
        for m, right in enumerate((d0, d1, d2, d3)):
            below[...] = right[size:, :].astype(F32)
            for i in range(TAPS):
                cover[m * groups : (m + 1) * groups, i * width : (i + 1) * width] = below[
                    i * groups : (i + 1) * groups, :
                ]

    return call(
        body,
        place,
        local([earlier, own, later] + cots),
        [like((half, cols), F32), like((half, cols), BF), like((NY * groups, cols), F32), like((8, 128), F32)],
        scratch=[pltpu.VMEM((EXTRA, width), F32), pltpu.VMEM((TAPS, NY * size, width), BF)],
        after=after,
        flops=2 * size * NY * width * cols,
        moved=8 * NY * width * size,
    )


def over_z(place, kept, came, cover, after):
    rows, cols = kept.shape

    def body(place, kept, came, cover, *refs):
        outs, total, message = refs[:NZ], refs[NZ], refs[NZ + 1]
        total[...] = kept[...] + came[...].astype(F32)
        message[:EXTRA, :] = cover[...]
        for m, ref in enumerate(outs):
            at = pl.multiple_of(lax.rem(place[2] + m, NZ) * GROUP, 8)
            if m == 0:
                ref[...] = total[pl.ds(at, GROUP), :]
            else:
                message[EXTRA:, :] = total[pl.ds(at, GROUP), :]
                ref[...] = message[...].astype(BF)

    return call(
        body,
        place,
        local([kept, came, cover]),
        [like((GROUP, cols), F32)] + [like((EXTRA + GROUP, cols), BF)] * (NZ - 1),
        scratch=[pltpu.VMEM((rows, cols), F32), pltpu.VMEM((EXTRA + GROUP, cols), F32)],
        after=after,
        flops=4 * rows * cols,
        moved=6 * rows * cols,
    )


def summed(place, kept, cover, parts, wide):
    rows, cols = kept.shape
    width = cols // TAPS

    def body(place, kept, cover, *refs):
        parts, (out, blocks, done) = refs[: NZ - 1], refs[NZ - 1 :]
        done[...] = jnp.zeros_like(done)
        total = kept[...]
        blocks[0] = cover[:, :wide].astype(BF)
        for m, part in enumerate(parts):
            total += part[...].astype(F32)[EXTRA:]
            blocks[m + 1] = part[:EXTRA, :wide]
        for k in range(TAPS):
            out[k] = total[:, k * width : (k + 1) * width]

    return call(
        body,
        place,
        local([kept, cover] + parts),
        [like((TAPS, rows, width), F32), like((NZ, EXTRA, wide), BF), like((8, 128), F32)],
        flops=NZ * rows * cols,
        moved=2 * NZ * (rows + EXTRA) * cols,
    )


def input_gradient(place, inputs, grad, own, came, after):
    def body(place, state, grad, own, c1, c2, c3, out, done):
        back_u = own[...] + c1[...].astype(F32) + c2[...].astype(F32) + c3[...].astype(F32)
        out[...] = (grad[...] + activation_slope(state[...].astype(F32), back_u)).astype(BF)
        done[...] = jnp.zeros_like(done)

    return call(
        body,
        place,
        local([inputs, grad, own] + came),
        [like(inputs.shape, BF), like((8, 128), F32)],
        after=after,
        flops=20 * inputs.size,
        moved=16 * inputs.size,
    )


def coverage_of(blocks, place, exon_blocks, own):
    _, y, z, core = (place[i] for i in range(4))
    flip, dz, dy, part = jnp.meshgrid(
        *(jnp.arange(n, dtype=jnp.int32) for n in (2, NZ, NY, own)), indexing="ij"
    )
    labels = seq_index((y + NY - dy) % NY, (z + NZ - dz) % NZ, core ^ flip) * own + part
    labels = labels.reshape(-1)
    counts = (exon_blocks[:, :, None] == labels[None, None]).astype(F32).sum(axis=1)
    total = jnp.dot(
        counts.astype(BF), blocks.reshape(labels.shape[0], -1), preferred_element_type=F32
    )
    return total / jnp.sqrt(F32(EXONS * BLOCK))


def shards(inputs, conv_weight, head_weight, head_cot, exon_blocks):
    size, width = inputs.shape
    wide = head_cot.shape[1]
    own = size // BLOCK
    x = lax.axis_index("chan")
    s = lax.axis_index("seq")
    core, z, y = s % 2, (s // 2) % NZ, s // (2 * NZ)
    place = jnp.stack([x, y, z, core]).astype(jnp.int32)
    steps = 2

    state = inputs.astype(F32)
    acted = from_all_x(jax.nn.gelu(state).astype(BF))
    (taps,) = load(place, [conv_weight], (token(acted[0]),))
    low, mid, up, whole = conv_products(place, acted, taps, ())
    low, up = shifted(low, steps), shifted(up, -steps)
    after_conv = (state + (mid + low.astype(F32) + up.astype(F32))).astype(BF)
    full = from_all_x(after_conv)
    turned = turned_blocks(place, whole, (token(after_conv),))
    turned = [turned[0]] + [along_seq(turned[m], m, 0, 0) for m in range(1, NY)]

    head, cot = load(place, [head_weight, head_cot], (token(after_conv),))
    tracks, sums, *blocks, done = track_head(place, full, head, cot, ())
    turned = stacked(place, turned, (done,))
    before = along_seq(turned, 0, 1, 0)
    behind = along_seq(turned, 0, NZ - 1, 0)
    came = [along_x(blocks[r], r) for r in range(1, NX)]
    (taps,) = load(place, [conv_weight], (done,))
    grad, low, long = add_up(place, blocks[0], came, sums, ())

    cots = [long] + [along_seq(long, m, 0, 0) for m in range(1, NY)]
    around = [shifted(low, -steps), low, shifted(low, steps)]
    kept, sent, cover, done = kernel_terms(place, before, turned, behind, cots, own, ())
    *blocks, done = back_products(place, around, taps, (done,))
    came = [along_x(blocks[r], r) for r in range(1, NX)]
    kept, *parts = over_z(place, kept, along_seq(sent, 0, 0, 1), cover, (done,))
    parts = [along_seq(part, 0, m + 1, 0) for m, part in enumerate(parts)]
    kernel_gradient, cover, done = summed(place, kept, cover, parts, wide)
    out, _ = input_gradient(place, inputs, grad, blocks[0], came, (done,))
    cover = jnp.stack([cover, along_seq(cover, 0, 0, 1)])
    coverage = coverage_of(cover, place, exon_blocks, own)
    return (tracks, coverage, out, kernel_gradient[None])


def solution(mesh):
    return jax.shard_map(
        shards,
        mesh=mesh,
        in_specs=(
            P("seq", "chan"),
            P(None, None, None, "chan"),
            P(None, "chan"),
            P("seq", "chan"),
            P("seq", None),
        ),
        out_specs=(
            P("seq", "chan"),
            P("seq", "chan"),
            P("seq", "chan"),
            P(None, None, "seq", "chan"),
        ),
        check_vma=False,
    )
```

```python
import jax
import jax.numpy as jnp
from jax import lax
from jax.experimental import pallas as pl
from jax.experimental.pallas import tpu as pltpu
from jax.sharding import PartitionSpec as P

BLOCK = 128
EXONS = 8
NX, NY, NZ = 4, 4, 8
TAPS = 3
GROUP = 24
F32 = jnp.float32
BF = jnp.bfloat16


def activation_slope(point, cotan):
    _, back = jax.vjp(jax.nn.gelu, point)
    return back(cotan)[0]


def seq_index(y, z, core):
    return (y * NZ + z) * 2 + core


def shifted(value, steps):
    count = lax.axis_size("seq")
    leading, last = (max(0, -steps), min(count, count - steps))
    return lax.ppermute(value, "seq", [(s, s + steps) for s in range(leading, last)])


def along_x(value, steps):
    return lax.ppermute(value, "chan", [(i, (i + steps) % NX) for i in range(NX)])


def along_seq(value, dy, dz, dcore):
    pairs = [
        (
            seq_index(y, z, core),
            seq_index((y + dy) % NY, (z + dz) % NZ, (core + dcore) % 2),
        )
        for y in range(NY)
        for z in range(NZ)
        for core in range(2)
    ]
    return lax.ppermute(value, "seq", pairs)


def from_all_x(value):
    return [value] + [along_x(value, -r) for r in range(1, NX)]


def times_t(left, right):
    return lax.dot_general(left, right, (((1,), (1,)), ((), ())), preferred_element_type=F32)


def call(body, place, operands, outs, scratch=(), after=(), limit=12, flops=0, moved=0):
    count = len(operands)

    def kernel(*refs):
        body(refs[0], *refs[1 : 1 + count], *refs[1 + count + len(after) :])

    vmem = pl.BlockSpec(memory_space=pltpu.VMEM)
    return pl.pallas_call(
        kernel,
        in_specs=[pl.BlockSpec(memory_space=pltpu.SMEM)]
        + [pl.BlockSpec(memory_space=space) for _, space in operands]
        + [pl.BlockSpec(memory_space=pl.ANY)] * len(after),
        out_specs=[vmem] * len(outs),
        scratch_shapes=list(scratch),
        out_shape=outs,
        cost_estimate=pl.CostEstimate(flops=flops, bytes_accessed=moved, transcendentals=0),
        compiler_params=pltpu.CompilerParams(vmem_limit_bytes=limit * 2**20),
    )(place, *[value for value, _ in operands], *after)


def local(values):
    return [(value, pltpu.VMEM) for value in values]


def like(shape, dtype):
    return jax.ShapeDtypeStruct(shape, dtype)


def slot(place, r, width):
    return pl.ds(pl.multiple_of(lax.rem(place[0] + r, NX) * width, 128), width)


def conv_products(place, blocks, conv_weight, after):
    size, width = blocks[0].shape
    tall = NX * width

    def body(place, b0, b1, b2, b3, weight, low, mid, up, whole):
        for r, block in enumerate((b0, b1, b2, b3)):
            whole[:, slot(place, r, width)] = block[...]
        for k, ref in ((0, low), (2, up), (1, mid)):
            product = jnp.dot(whole[...], weight[0, k], preferred_element_type=F32)
            ref[...] = product.astype(ref.dtype)

    block = (size, width)
    return call(
        body,
        place,
        local(blocks + [conv_weight]),
        [like(block, BF), like(block, F32), like(block, BF), like((size, tall), BF)],
        after=after,
        flops=2 * size * tall * TAPS * width,
        moved=2 * tall * TAPS * width,
    )


def load(place, values, after):
    count = len(values)

    def body(place, *refs):
        sems = refs[-1]
        copies = [pltpu.make_async_copy(refs[i], refs[count + i], sems.at[i]) for i in range(count)]
        for copy in copies:
            copy.start()
        for copy in copies:
            copy.wait()

    return call(
        body,
        place,
        [(value, pl.ANY) for value in values],
        [like(value.shape, value.dtype) for value in values],
        scratch=[pltpu.SemaphoreType.DMA((count,))],
        after=after,
        limit=4,
        moved=sum(4 * value.size for value in values),
    )


def turned_blocks(place, whole, after):
    size, tall = whole.shape
    width = tall // NY

    def body(place, whole, *outs):
        for m, out in enumerate(outs):
            at = pl.multiple_of(lax.rem(place[1] + m, NY) * width, 128)
            out[...] = whole[:, pl.ds(at, width)].T

    return call(
        body,
        place,
        local([whole]),
        [like((width, size), BF)] * NY,
        after=after,
        flops=size * tall,
        limit=4,
        moved=4 * size * tall,
    )


def stacked(place, values, after):
    rows, cols = values[0].shape

    def body(place, *refs):
        for i in range(len(values)):
            refs[-1][:, i * cols : (i + 1) * cols] = refs[i][...]

    return call(
        body,
        place,
        local(values),
        [like((rows, len(values) * cols), BF)],
        after=after,
        limit=4,
        moved=4 * len(values) * values[0].size,
    )[0]


def token(value):
    return value[(0,) * (value.ndim - 2) + (slice(8), slice(128))]


def track_head(place, blocks, head_weight, head_cot, after):
    size, width = blocks[0].shape
    tall, wide = head_weight.shape
    tile = 256
    groups = size // BLOCK

    def body(place, b0, b1, b2, b3, weight, cot, out, sums, o0, o1, o2, o3, done, whole, term):
        for r, block in enumerate((b0, b1, b2, b3)):
            whole[:, slot(place, r, width)] = block[...]
        for j in range(wide // tile):
            cols = slice(j * tile, (j + 1) * tile)
            logits = jnp.dot(whole[...], weight[:, cols], preferred_element_type=F32)
            decay = jnp.exp(-jnp.abs(logits))
            above = 1.0 + decay
            log = jnp.where(decay < 1e-3, decay - 0.5 * decay * decay, jnp.log(above))
            track = (jnp.maximum(logits, 0.0) + log).astype(BF)
            out[:, cols] = track
            sums[:, cols] = jnp.sum(track.astype(F32).reshape(groups, BLOCK, tile), axis=1)
            part = pl.reciprocal(above, approx=True)
            part = part * (2.0 - above * part)
            sigmoid = jnp.where(logits >= 0.0, part, decay * part)
            term[:, cols] = (cot[:, cols].astype(F32) * sigmoid).astype(BF)
        for r, ref in ((2, o2), (1, o1), (3, o3), (0, o0)):
            ref[...] = times_t(term[...], weight[slot(place, r, width), :]).astype(ref.dtype)
        done[...] = jnp.zeros_like(done)

    block = (size, width)
    return call(
        body,
        place,
        local(blocks + [head_weight, head_cot]),
        [like((size, wide), BF), like((groups, wide), F32), like(block, F32)] + [like(block, BF)] * 3 + [like((8, 128), F32)],
        scratch=[pltpu.VMEM((size, tall), BF), pltpu.VMEM((size, wide), BF)],
        after=after,
        flops=4 * size * tall * wide,
        moved=2 * tall * wide,
    )


EXTRA = 16


def add_up(place, own, came, sums, after):
    size, width = own.shape
    groups, wide = sums.shape

    def body(place, own, c1, c2, c3, sums, total, low, long, below):
        value = own[...] + c1[...].astype(F32) + c2[...].astype(F32) + c3[...].astype(F32)
        total[...] = value
        low[...] = value.astype(BF)
        long[:size, :] = value.astype(BF)
        below[...] = jnp.zeros((EXTRA, width), F32)
        for i in range(TAPS):
            cols = min(width, wide - i * width)
            below[i * groups : (i + 1) * groups, :cols] = sums[:, i * width : i * width + cols]
        long[size:, :] = below[...].astype(BF)

    return call(
        body,
        place,
        local([own] + came + [sums]),
        [like((size, width), F32), like((size, width), BF), like((size + EXTRA, width), BF)],
        scratch=[pltpu.VMEM((EXTRA, width), F32)],
        after=after,
        flops=4 * own.size,
        limit=4,
        moved=16 * own.size,
    )


def back_products(place, around, conv_weight, after):
    size, width = around[0].shape
    tall = NX * width
    cols = TAPS * width

    def body(place, d0, d1, d2, weight, o0, o1, o2, o3, done):
        for r, ref in ((2, o2), (1, o1), (3, o3), (0, o0)):
            at = slot(place, r, width)
            total = times_t(d0[...], weight[0, 0, at, :])
            total += times_t(d1[...], weight[0, 1, at, :])
            total += times_t(d2[...], weight[0, 2, at, :])
            ref[...] = total.astype(ref.dtype)
        done[...] = jnp.zeros_like(done)

    block = (size, width)
    return call(
        body,
        place,
        local(around + [conv_weight]),
        [like(block, F32)] + [like(block, BF)] * 3 + [like((8, 128), F32)],
        after=after,
        flops=2 * size * tall * cols,
        moved=2 * tall * cols,
    )


def kernel_terms(place, earlier, own, later, cots, groups, after):
    width, size = own.shape[0], own.shape[1] // NY
    half = width // 2
    cols = TAPS * width

    def body(place, earlier, own, later, d0, d1, d2, d3, kept, sent, cover, done, below, joined):
        y, z, core = place[1], place[2], place[3]
        first, last = z == 0, z == NZ - 1
        done[...] = jnp.zeros_like(done)
        for k, left in enumerate((earlier, own, later)):
            for m, right in enumerate((d0, d1, d2, d3)):
                if k == 0:
                    index = jnp.where(first, (m + 1) % NY, m)
                    valid = jnp.logical_not(jnp.logical_and(first, y == m))
                elif k == 2:
                    index = jnp.where(last, (m + NY - 1) % NY, m)
                    valid = jnp.logical_not(jnp.logical_and(last, y == (m + NY - 1) % NY))
                else:
                    joined[k, m * size : (m + 1) * size, :] = right[:size, :]
                    continue
                at = pl.ds(pl.multiple_of(index * size, size), size)

                @pl.when(valid)
                def _():
                    joined[k, at, :] = right[:size, :]

                @pl.when(jnp.logical_not(valid))
                def _():
                    joined[k, at, :] = jnp.zeros((size, width), BF)

        for k, left in enumerate((earlier, own, later)):
            total = jnp.dot(left[...], joined[k], preferred_element_type=F32)
            pairs = total.reshape(half // GROUP, 2, GROUP, width)
            one, two = (pairs[:, i].reshape(half, width) for i in range(2))
            at = slice(k * width, (k + 1) * width)
            kept[:, at] = jnp.where(core == 0, one, two)
            sent[:, at] = jnp.where(core == 0, two, one).astype(BF)
        for m, right in enumerate((d0, d1, d2, d3)):
            below[...] = right[size:, :].astype(F32)
            for i in range(TAPS):
                cover[m * groups : (m + 1) * groups, i * width : (i + 1) * width] = below[
                    i * groups : (i + 1) * groups, :
                ]

    return call(
        body,
        place,
        local([earlier, own, later] + cots),
        [like((half, cols), F32), like((half, cols), BF), like((NY * groups, cols), F32), like((8, 128), F32)],
        scratch=[pltpu.VMEM((EXTRA, width), F32), pltpu.VMEM((TAPS, NY * size, width), BF)],
        after=after,
        flops=2 * size * NY * width * cols,
        moved=8 * NY * width * size,
    )


def over_z(place, kept, came, cover, after):
    rows, cols = kept.shape

    def body(place, kept, came, cover, *refs):
        outs, total, message = refs[:NZ], refs[NZ], refs[NZ + 1]
        total[...] = kept[...] + came[...].astype(F32)
        message[:EXTRA, :] = cover[...]
        for m, ref in enumerate(outs):
            at = pl.multiple_of(lax.rem(place[2] + m, NZ) * GROUP, 8)
            if m == 0:
                ref[...] = total[pl.ds(at, GROUP), :]
            else:
                message[EXTRA:, :] = total[pl.ds(at, GROUP), :]
                ref[...] = message[...].astype(BF)

    return call(
        body,
        place,
        local([kept, came, cover]),
        [like((GROUP, cols), F32)] + [like((EXTRA + GROUP, cols), BF)] * (NZ - 1),
        scratch=[pltpu.VMEM((rows, cols), F32), pltpu.VMEM((EXTRA + GROUP, cols), F32)],
        after=after,
        flops=4 * rows * cols,
        limit=4,
        moved=6 * rows * cols,
    )


def summed(place, kept, cover, parts, wide, after):
    rows, cols = kept.shape
    width = cols // TAPS

    def body(place, kept, cover, *refs):
        parts, (out, blocks, done) = refs[: NZ - 1], refs[NZ - 1 :]
        done[...] = jnp.zeros_like(done)
        total = kept[...]
        blocks[0] = cover[:, :wide].astype(BF)
        for m, part in enumerate(parts):
            total += part[...].astype(F32)[EXTRA:]
            blocks[m + 1] = part[:EXTRA, :wide]
        for k in range(TAPS):
            out[k] = total[:, k * width : (k + 1) * width]

    return call(
        body,
        place,
        local([kept, cover] + parts),
        [like((TAPS, rows, width), F32), like((NZ, EXTRA, wide), BF), like((8, 128), F32)],
        after=after,
        flops=NZ * rows * cols,
        limit=4,
        moved=2 * NZ * (rows + EXTRA) * cols,
    )


def input_gradient(place, inputs, grad, own, came, after):
    def body(place, state, grad, own, c1, c2, c3, out, done):
        back_u = own[...] + c1[...].astype(F32) + c2[...].astype(F32) + c3[...].astype(F32)
        out[...] = (grad[...] + activation_slope(state[...].astype(F32), back_u)).astype(BF)
        done[...] = jnp.zeros_like(done)

    return call(
        body,
        place,
        local([inputs, grad, own] + came),
        [like(inputs.shape, BF), like((8, 128), F32)],
        after=after,
        flops=20 * inputs.size,
        limit=4,
        moved=16 * inputs.size,
    )


def counts_of(place, exon_blocks, own):
    _, y, z, core = (place[i] for i in range(4))
    flip, dz, dy, part = jnp.meshgrid(
        *(jnp.arange(n, dtype=jnp.int32) for n in (2, NZ, NY, own)), indexing="ij"
    )
    labels = seq_index((y + NY - dy) % NY, (z + NZ - dz) % NZ, core ^ flip) * own + part
    labels = labels.reshape(-1)
    return (exon_blocks[:, :, None] == labels[None, None]).astype(F32).sum(axis=1).astype(BF)


def coverage_of(blocks, counts):
    blocks = blocks.reshape(counts.shape[1], -1)
    total = jnp.dot(counts, blocks, preferred_element_type=F32)
    return total / jnp.sqrt(F32(EXONS * BLOCK))


def shards(inputs, conv_weight, head_weight, head_cot, exon_blocks):
    size, width = inputs.shape
    wide = head_cot.shape[1]
    own = size // BLOCK
    x = lax.axis_index("chan")
    s = lax.axis_index("seq")
    core, z, y = s % 2, (s // 2) % NZ, s // (2 * NZ)
    place = jnp.stack([x, y, z, core]).astype(jnp.int32)
    steps = 2

    state = inputs.astype(F32)
    acted = from_all_x(jax.nn.gelu(state).astype(BF))
    counts = counts_of(place, exon_blocks, own)
    (taps,) = load(place, [conv_weight], (token(acted[0]), counts))
    low, mid, up, whole = conv_products(place, acted, taps, ())
    low, up = shifted(low, steps), shifted(up, -steps)
    after_conv = (state + (mid + low.astype(F32) + up.astype(F32))).astype(BF)
    full = from_all_x(after_conv)
    turned = turned_blocks(place, whole, (token(after_conv),))
    turned = [turned[0]] + [along_seq(turned[m], m, 0, 0) for m in range(1, NY)]

    head, cot = load(place, [head_weight, head_cot], (token(after_conv),))
    tracks, sums, *blocks, done = track_head(place, full, head, cot, ())
    turned = stacked(place, turned, (done,))
    before = along_seq(turned, 0, 1, 0)
    behind = along_seq(turned, 0, NZ - 1, 0)
    came = [along_x(blocks[r], r) for r in range(1, NX)]
    (taps,) = load(place, [conv_weight], (done,))
    grad, low, long = add_up(place, blocks[0], came, sums, ())

    cots = [long] + [along_seq(long, m, 0, 0) for m in range(1, NY)]
    around = [shifted(low, -steps), low, shifted(low, steps)]
    kept, sent, cover, done = kernel_terms(place, before, turned, behind, cots, own, ())
    *blocks, done = back_products(place, around, taps, (done,))
    came = [along_x(blocks[r], r) for r in range(1, NX)]
    kept, *parts = over_z(place, kept, along_seq(sent, 0, 0, 1), cover, (done,))
    parts = [along_seq(part, 0, m + 1, 0) for m, part in enumerate(parts)]
    out, done = input_gradient(place, inputs, grad, blocks[0], came, ())
    kernel_gradient, cover, _ = summed(place, kept, cover, parts, wide, (done,))
    cover = jnp.stack([cover, along_seq(cover, 0, 0, 1)])
    coverage = coverage_of(cover, counts)
    return (tracks, coverage, out, kernel_gradient[None])


def solution(mesh):
    return jax.shard_map(
        shards,
        mesh=mesh,
        in_specs=(
            P("seq", "chan"),
            P(None, None, None, "chan"),
            P(None, "chan"),
            P("seq", "chan"),
            P("seq", None),
        ),
        out_specs=(
            P("seq", "chan"),
            P("seq", "chan"),
            P("seq", "chan"),
            P(None, None, "seq", "chan"),
        ),
        check_vma=False,
    )
```

```python
import jax
import jax.numpy as jnp
from jax import lax
from jax.experimental import pallas as pl
from jax.experimental.pallas import tpu as pltpu
from jax.sharding import PartitionSpec as P

BLOCK = 128
EXONS = 8
NX, NY, NZ = 4, 4, 8
TAPS = 3
GROUP = 24
F32 = jnp.float32
BF = jnp.bfloat16


def activation_slope(point, cotan):
    _, back = jax.vjp(jax.nn.gelu, point)
    return back(cotan)[0]


def seq_index(y, z, core):
    return (y * NZ + z) * 2 + core


def shifted(value, steps):
    count = lax.axis_size("seq")
    leading, last = (max(0, -steps), min(count, count - steps))
    return lax.ppermute(value, "seq", [(s, s + steps) for s in range(leading, last)])


def along_x(value, steps):
    return lax.ppermute(value, "chan", [(i, (i + steps) % NX) for i in range(NX)])


def along_seq(value, dy, dz, dcore):
    pairs = [
        (
            seq_index(y, z, core),
            seq_index((y + dy) % NY, (z + dz) % NZ, (core + dcore) % 2),
        )
        for y in range(NY)
        for z in range(NZ)
        for core in range(2)
    ]
    return lax.ppermute(value, "seq", pairs)


def from_all_x(value):
    return [value] + [along_x(value, -r) for r in range(1, NX)]


def times_t(left, right):
    return lax.dot_general(left, right, (((1,), (1,)), ((), ())), preferred_element_type=F32)


def call(body, place, operands, outs, scratch=(), after=(), limit=12, flops=0, moved=0):
    count = len(operands)

    def kernel(*refs):
        body(refs[0], *refs[1 : 1 + count], *refs[1 + count + len(after) :])

    vmem = pl.BlockSpec(memory_space=pltpu.VMEM)
    return pl.pallas_call(
        kernel,
        in_specs=[pl.BlockSpec(memory_space=pltpu.SMEM)]
        + [pl.BlockSpec(memory_space=space) for _, space in operands]
        + [pl.BlockSpec(memory_space=pl.ANY)] * len(after),
        out_specs=[vmem] * len(outs),
        scratch_shapes=list(scratch),
        out_shape=outs,
        cost_estimate=pl.CostEstimate(flops=flops, bytes_accessed=moved, transcendentals=0),
        compiler_params=pltpu.CompilerParams(vmem_limit_bytes=limit * 2**20),
    )(place, *[value for value, _ in operands], *after)


def local(values):
    return [(value, pltpu.VMEM) for value in values]


def like(shape, dtype):
    return jax.ShapeDtypeStruct(shape, dtype)


def slot(place, r, width):
    return pl.ds(pl.multiple_of(lax.rem(place[0] + r, NX) * width, 128), width)


def conv_products(place, blocks, conv_weight, after):
    size, width = blocks[0].shape
    tall = NX * width

    def body(place, b0, b1, b2, b3, weight, low, mid, up, whole):
        for r, block in enumerate((b0, b1, b2, b3)):
            whole[:, slot(place, r, width)] = block[...]
        for k, ref in ((0, low), (2, up), (1, mid)):
            product = jnp.dot(whole[...], weight[0, k], preferred_element_type=F32)
            ref[...] = product.astype(ref.dtype)

    block = (size, width)
    return call(
        body,
        place,
        local(blocks + [conv_weight]),
        [like(block, BF), like(block, F32), like(block, BF), like((size, tall), BF)],
        after=after,
        flops=2 * size * tall * TAPS * width,
        moved=2 * tall * TAPS * width,
    )


def load(place, values, after):
    count = len(values)

    def body(place, *refs):
        sems = refs[-1]
        copies = [pltpu.make_async_copy(refs[i], refs[count + i], sems.at[i]) for i in range(count)]
        for copy in copies:
            copy.start()
        for copy in copies:
            copy.wait()

    return call(
        body,
        place,
        [(value, pl.ANY) for value in values],
        [like(value.shape, value.dtype) for value in values],
        scratch=[pltpu.SemaphoreType.DMA((count,))],
        after=after,
        limit=4,
        moved=sum(4 * value.size for value in values),
    )


def turned_blocks(place, whole, after):
    size, tall = whole.shape
    width = tall // NY

    def body(place, whole, *outs):
        for m, out in enumerate(outs):
            at = pl.multiple_of(lax.rem(place[1] + m, NY) * width, 128)
            out[...] = whole[:, pl.ds(at, width)].T

    return call(
        body,
        place,
        local([whole]),
        [like((width, size), BF)] * NY,
        after=after,
        flops=size * tall,
        limit=4,
        moved=4 * size * tall,
    )


def stacked(place, values, after):
    rows, cols = values[0].shape

    def body(place, *refs):
        for i in range(len(values)):
            refs[-1][:, i * cols : (i + 1) * cols] = refs[i][...]

    return call(
        body,
        place,
        local(values),
        [like((rows, len(values) * cols), BF)],
        after=after,
        limit=4,
        moved=4 * len(values) * values[0].size,
    )[0]


def token(value):
    return value[(0,) * (value.ndim - 2) + (slice(8), slice(128))]


def track_head(place, blocks, head_weight, head_cot, after):
    size, width = blocks[0].shape
    tall, wide = head_weight.shape
    tile = 256
    groups = size // BLOCK

    def body(place, b0, b1, b2, b3, weight, cot, out, sums, o0, o1, o2, o3, done, whole, term):
        for r, block in enumerate((b0, b1, b2, b3)):
            whole[:, slot(place, r, width)] = block[...]
        for j in range(wide // tile):
            cols = slice(j * tile, (j + 1) * tile)
            logits = jnp.dot(whole[...], weight[:, cols], preferred_element_type=F32)
            decay = jnp.exp(-jnp.abs(logits))
            above = 1.0 + decay
            log = jnp.where(decay < 1e-3, decay - 0.5 * decay * decay, jnp.log(above))
            track = (jnp.maximum(logits, 0.0) + log).astype(BF)
            out[:, cols] = track
            sums[:, cols] = jnp.sum(track.astype(F32).reshape(groups, BLOCK, tile), axis=1)
            part = pl.reciprocal(above, approx=True)
            part = part * (2.0 - above * part)
            sigmoid = jnp.where(logits >= 0.0, part, decay * part)
            term[:, cols] = (cot[:, cols].astype(F32) * sigmoid).astype(BF)
        for r, ref in ((2, o2), (1, o1), (3, o3), (0, o0)):
            ref[...] = times_t(term[...], weight[slot(place, r, width), :]).astype(ref.dtype)
        done[...] = jnp.zeros_like(done)

    block = (size, width)
    return call(
        body,
        place,
        local(blocks + [head_weight, head_cot]),
        [like((size, wide), BF), like((groups, wide), F32), like(block, F32)] + [like(block, BF)] * 3 + [like((8, 128), F32)],
        scratch=[pltpu.VMEM((size, tall), BF), pltpu.VMEM((size, wide), BF)],
        after=after,
        flops=4 * size * tall * wide,
        moved=2 * tall * wide,
    )


EXTRA = 16


def add_up(place, own, came, sums, after):
    size, width = own.shape
    groups, wide = sums.shape

    def body(place, own, c1, c2, c3, sums, total, low, long, below):
        value = own[...] + c1[...].astype(F32) + c2[...].astype(F32) + c3[...].astype(F32)
        total[...] = value
        low[...] = value.astype(BF)
        long[:size, :] = value.astype(BF)
        below[...] = jnp.zeros((EXTRA, width), F32)
        for i in range(TAPS):
            cols = min(width, wide - i * width)
            below[i * groups : (i + 1) * groups, :cols] = sums[:, i * width : i * width + cols]
        long[size:, :] = below[...].astype(BF)

    return call(
        body,
        place,
        local([own] + came + [sums]),
        [like((size, width), F32), like((size, width), BF), like((size + EXTRA, width), BF)],
        scratch=[pltpu.VMEM((EXTRA, width), F32)],
        after=after,
        flops=4 * own.size,
        limit=4,
        moved=16 * own.size,
    )


def back_products(place, around, conv_weight, after):
    size, width = around[0].shape
    tall = NX * width
    cols = TAPS * width

    def body(place, d0, d1, d2, weight, o0, o1, o2, o3, done):
        for r, ref in ((2, o2), (1, o1), (3, o3), (0, o0)):
            at = slot(place, r, width)
            total = times_t(d0[...], weight[0, 0, at, :])
            total += times_t(d1[...], weight[0, 1, at, :])
            total += times_t(d2[...], weight[0, 2, at, :])
            ref[...] = total.astype(ref.dtype)
        done[...] = jnp.zeros_like(done)

    block = (size, width)
    return call(
        body,
        place,
        local(around + [conv_weight]),
        [like(block, F32)] + [like(block, BF)] * 3 + [like((8, 128), F32)],
        after=after,
        flops=2 * size * tall * cols,
        moved=2 * tall * cols,
    )


def kernel_terms(place, earlier, own, later, cots, groups, after):
    width, size = own.shape[0], own.shape[1] // NY
    half = width // 2
    cols = TAPS * width

    def body(place, earlier, own, later, d0, d1, d2, d3, kept, sent, cover, done, below, joined):
        y, z, core = place[1], place[2], place[3]
        first, last = z == 0, z == NZ - 1
        done[...] = jnp.zeros_like(done)
        for k, left in enumerate((earlier, own, later)):
            for m, right in enumerate((d0, d1, d2, d3)):
                if k == 0:
                    index = jnp.where(first, (m + 1) % NY, m)
                    valid = jnp.logical_not(jnp.logical_and(first, y == m))
                elif k == 2:
                    index = jnp.where(last, (m + NY - 1) % NY, m)
                    valid = jnp.logical_not(jnp.logical_and(last, y == (m + NY - 1) % NY))
                else:
                    joined[k, m * size : (m + 1) * size, :] = right[:size, :]
                    continue
                at = pl.ds(pl.multiple_of(index * size, size), size)

                @pl.when(valid)
                def _():
                    joined[k, at, :] = right[:size, :]

                @pl.when(jnp.logical_not(valid))
                def _():
                    joined[k, at, :] = jnp.zeros((size, width), BF)

        for k, left in enumerate((earlier, own, later)):
            total = jnp.dot(left[...], joined[k], preferred_element_type=F32)
            pairs = total.reshape(half // GROUP, 2, GROUP, width)
            one, two = (pairs[:, i].reshape(half, width) for i in range(2))
            at = slice(k * width, (k + 1) * width)
            kept[:, at] = jnp.where(core == 0, one, two)
            sent[:, at] = jnp.where(core == 0, two, one).astype(BF)
        for m, right in enumerate((d0, d1, d2, d3)):
            below[...] = right[size:, :].astype(F32)
            for i in range(TAPS):
                cover[m * groups : (m + 1) * groups, i * width : (i + 1) * width] = below[
                    i * groups : (i + 1) * groups, :
                ]

    return call(
        body,
        place,
        local([earlier, own, later] + cots),
        [like((half, cols), F32), like((half, cols), BF), like((NY * groups, cols), F32), like((8, 128), F32)],
        scratch=[pltpu.VMEM((EXTRA, width), F32), pltpu.VMEM((TAPS, NY * size, width), BF)],
        after=after,
        flops=2 * size * NY * width * cols,
        moved=8 * NY * width * size,
    )


def over_z(place, kept, came, cover, after):
    rows, cols = kept.shape

    def body(place, kept, came, cover, out, message):
        total = kept[...] + came[...].astype(F32)
        message[:EXTRA, :] = cover[...]
        for z in range(NZ):
            message[EXTRA:, :] = total[z * GROUP : (z + 1) * GROUP, :]
            out[z] = message[...].astype(BF)

    return call(
        body,
        place,
        local([kept, came, cover]),
        [like((NZ, EXTRA + GROUP, cols), BF)],
        scratch=[pltpu.VMEM((EXTRA + GROUP, cols), F32)],
        after=after,
        flops=4 * rows * cols,
        moved=6 * rows * cols,
        limit=8,
    )[0]


def summed(place, parts, wide, after):
    _, rows, cols = parts.shape
    rows = rows - EXTRA
    width = cols // TAPS

    def body(place, parts, out, blocks):
        total = jnp.zeros((rows, cols), F32)
        for z in range(NZ):
            total += parts[z].astype(F32)[EXTRA:]
            blocks[z] = parts[z, :EXTRA, :wide]
        for k in range(TAPS):
            out[k] = total[:, k * width : (k + 1) * width]

    return call(
        body,
        place,
        local([parts]),
        [like((TAPS, rows, width), F32), like((NZ, EXTRA, wide), BF)],
        after=after,
        flops=NZ * rows * cols,
        moved=2 * NZ * (rows + EXTRA) * cols,
        limit=8,
    )


def input_gradient(place, inputs, grad, own, came, after):
    def body(place, state, grad, own, c1, c2, c3, out, done):
        back_u = own[...] + c1[...].astype(F32) + c2[...].astype(F32) + c3[...].astype(F32)
        out[...] = (grad[...] + activation_slope(state[...].astype(F32), back_u)).astype(BF)
        done[...] = jnp.zeros_like(done)

    return call(
        body,
        place,
        local([inputs, grad, own] + came),
        [like(inputs.shape, BF), like((8, 128), F32)],
        after=after,
        flops=20 * inputs.size,
        limit=4,
        moved=16 * inputs.size,
    )


def counts_of(place, exon_blocks, own):
    y, core = place[1], place[3]
    flip, dz, dy, part = jnp.meshgrid(
        *(jnp.arange(n, dtype=jnp.int32) for n in (2, NZ, NY, own)), indexing="ij"
    )
    labels = seq_index((y + NY - dy) % NY, dz, core ^ flip) * own + part
    labels = labels.reshape(-1)
    return (exon_blocks[:, :, None] == labels[None, None]).astype(F32).sum(axis=1).astype(BF)


def coverage_of(blocks, counts):
    blocks = blocks.reshape(counts.shape[1], -1)
    total = jnp.dot(counts, blocks, preferred_element_type=F32)
    return total / jnp.sqrt(F32(EXONS * BLOCK))


def shards(inputs, conv_weight, head_weight, head_cot, exon_blocks):
    size, width = inputs.shape
    wide = head_cot.shape[1]
    own = size // BLOCK
    x = lax.axis_index("chan")
    s = lax.axis_index("seq")
    core, z, y = s % 2, (s // 2) % NZ, s // (2 * NZ)
    place = jnp.stack([x, y, z, core]).astype(jnp.int32)
    steps = 2

    state = inputs.astype(F32)
    acted = from_all_x(jax.nn.gelu(state).astype(BF))
    counts = counts_of(place, exon_blocks, own)
    (taps,) = load(place, [conv_weight], (token(acted[0]), counts))
    low, mid, up, whole = conv_products(place, acted, taps, ())
    low, up = shifted(low, steps), shifted(up, -steps)
    after_conv = (state + (mid + low.astype(F32) + up.astype(F32))).astype(BF)
    full = from_all_x(after_conv)
    turned = turned_blocks(place, whole, (token(after_conv),))
    turned = [turned[0]] + [along_seq(turned[m], m, 0, 0) for m in range(1, NY)]

    head, cot = load(place, [head_weight, head_cot], (token(after_conv),))
    tracks, sums, *blocks, done = track_head(place, full, head, cot, ())
    turned = stacked(place, turned, (done,))
    before = along_seq(turned, 0, 1, 0)
    behind = along_seq(turned, 0, NZ - 1, 0)
    came = [along_x(blocks[r], r) for r in range(1, NX)]
    (taps,) = load(place, [conv_weight], (done,))
    grad, low, long = add_up(place, blocks[0], came, sums, ())

    cots = [long] + [along_seq(long, m, 0, 0) for m in range(1, NY)]
    around = [shifted(low, -steps), low, shifted(low, steps)]
    kept, sent, cover, done = kernel_terms(place, before, turned, behind, cots, own, ())
    *blocks, done = back_products(place, around, taps, (done,))
    came = [along_x(blocks[r], r) for r in range(1, NX)]
    parts = over_z(place, kept, along_seq(sent, 0, 0, 1), cover, (done,))
    groups = [[seq_index(j, i, c) for i in range(NZ)] for j in range(NY) for c in range(2)]
    parts = lax.all_to_all(parts, "seq", 0, 0, axis_index_groups=groups)
    out, done = input_gradient(place, inputs, grad, blocks[0], came, ())
    kernel_gradient, cover = summed(place, parts, wide, (done,))
    cover = jnp.stack([cover, along_seq(cover, 0, 0, 1)])
    coverage = coverage_of(cover, counts)
    return (tracks, coverage, out, kernel_gradient[None])


def solution(mesh):
    return jax.shard_map(
        shards,
        mesh=mesh,
        in_specs=(
            P("seq", "chan"),
            P(None, None, None, "chan"),
            P(None, "chan"),
            P("seq", "chan"),
            P("seq", None),
        ),
        out_specs=(
            P("seq", "chan"),
            P("seq", "chan"),
            P("seq", "chan"),
            P(None, None, "seq", "chan"),
        ),
        check_vma=False,
    )
```

```python
import jax
import jax.numpy as jnp
from jax import lax
from jax.experimental import pallas as pl
from jax.experimental.pallas import tpu as pltpu
from jax.sharding import PartitionSpec as P

BLOCK = 128
EXONS = 8
NX, NY, NZ = 4, 4, 8
TAPS = 3
GROUP = 24
F32 = jnp.float32
BF = jnp.bfloat16


def activation_slope(point, cotan):
    _, back = jax.vjp(jax.nn.gelu, point)
    return back(cotan)[0]


def seq_index(y, z, core):
    return (y * NZ + z) * 2 + core


def shifted(value, steps):
    count = lax.axis_size("seq")
    leading, last = (max(0, -steps), min(count, count - steps))
    return lax.ppermute(value, "seq", [(s, s + steps) for s in range(leading, last)])


def along_x(value, steps):
    return lax.ppermute(value, "chan", [(i, (i + steps) % NX) for i in range(NX)])


def along_seq(value, dy, dz, dcore):
    pairs = [
        (
            seq_index(y, z, core),
            seq_index((y + dy) % NY, (z + dz) % NZ, (core + dcore) % 2),
        )
        for y in range(NY)
        for z in range(NZ)
        for core in range(2)
    ]
    return lax.ppermute(value, "seq", pairs)


def from_all_x(value):
    return [value] + [along_x(value, -r) for r in range(1, NX)]


def times_t(left, right):
    return lax.dot_general(left, right, (((1,), (1,)), ((), ())), preferred_element_type=F32)


def call(body, place, operands, outs, scratch=(), after=(), limit=12, flops=0, moved=0):
    count = len(operands)

    def kernel(*refs):
        body(refs[0], *refs[1 : 1 + count], *refs[1 + count + len(after) :])

    vmem = pl.BlockSpec(memory_space=pltpu.VMEM)
    return pl.pallas_call(
        kernel,
        in_specs=[pl.BlockSpec(memory_space=pltpu.SMEM)]
        + [pl.BlockSpec(memory_space=space) for _, space in operands]
        + [pl.BlockSpec(memory_space=pl.ANY)] * len(after),
        out_specs=[vmem] * len(outs),
        scratch_shapes=list(scratch),
        out_shape=outs,
        cost_estimate=pl.CostEstimate(flops=flops, bytes_accessed=moved, transcendentals=0),
        compiler_params=pltpu.CompilerParams(vmem_limit_bytes=limit * 2**20),
    )(place, *[value for value, _ in operands], *after)


def local(values):
    return [(value, pltpu.VMEM) for value in values]


def like(shape, dtype):
    return jax.ShapeDtypeStruct(shape, dtype)


def slot(place, r, width):
    return pl.ds(pl.multiple_of(lax.rem(place[0] + r, NX) * width, 128), width)


def conv_products(place, blocks, conv_weight, after):
    size, width = blocks[0].shape
    tall = NX * width

    def body(place, b0, b1, b2, b3, weight, low, mid, up, whole):
        for r, block in enumerate((b0, b1, b2, b3)):
            whole[:, slot(place, r, width)] = block[...]
        for k, ref in ((0, low), (2, up), (1, mid)):
            product = jnp.dot(whole[...], weight[0, k], preferred_element_type=F32)
            ref[...] = product.astype(ref.dtype)

    block = (size, width)
    return call(
        body,
        place,
        local(blocks + [conv_weight]),
        [like(block, BF), like(block, F32), like(block, BF), like((size, tall), BF)],
        after=after,
        flops=2 * size * tall * TAPS * width,
        moved=2 * tall * TAPS * width,
    )


def load(place, values, after):
    count = len(values)

    def body(place, *refs):
        sems = refs[-1]
        copies = [pltpu.make_async_copy(refs[i], refs[count + i], sems.at[i]) for i in range(count)]
        for copy in copies:
            copy.start()
        for copy in copies:
            copy.wait()

    return call(
        body,
        place,
        [(value, pl.ANY) for value in values],
        [like(value.shape, value.dtype) for value in values],
        scratch=[pltpu.SemaphoreType.DMA((count,))],
        after=after,
        limit=4,
        moved=sum(4 * value.size for value in values),
    )


def turned_blocks(place, whole, after):
    size, tall = whole.shape
    width = tall // NY

    def body(place, whole, *outs):
        for m, out in enumerate(outs):
            at = pl.multiple_of(lax.rem(place[1] + m, NY) * width, 128)
            out[...] = whole[:, pl.ds(at, width)].T

    return call(
        body,
        place,
        local([whole]),
        [like((width, size), BF)] * NY,
        after=after,
        flops=size * tall,
        limit=4,
        moved=4 * size * tall,
    )


def stacked(place, values, after):
    rows, cols = values[0].shape

    def body(place, *refs):
        for i in range(len(values)):
            refs[-1][:, i * cols : (i + 1) * cols] = refs[i][...]

    return call(
        body,
        place,
        local(values),
        [like((rows, len(values) * cols), BF)],
        after=after,
        limit=4,
        moved=4 * len(values) * values[0].size,
    )[0]


def token(value):
    return value[(0,) * (value.ndim - 2) + (slice(8), slice(128))]


def track_head(place, blocks, head_weight, head_cot, after):
    size, width = blocks[0].shape
    tall, wide = head_weight.shape
    tile = 256
    groups = size // BLOCK

    def body(place, b0, b1, b2, b3, weight, cot, out, sums, o0, o1, o2, o3, done, whole, term):
        for r, block in enumerate((b0, b1, b2, b3)):
            whole[:, slot(place, r, width)] = block[...]
        for j in range(wide // tile):
            cols = slice(j * tile, (j + 1) * tile)
            logits = jnp.dot(whole[...], weight[:, cols], preferred_element_type=F32)
            decay = jnp.exp(-jnp.abs(logits))
            above = 1.0 + decay
            log = jnp.where(decay < 1e-3, decay - 0.5 * decay * decay, jnp.log(above))
            track = (jnp.maximum(logits, 0.0) + log).astype(BF)
            out[:, cols] = track
            sums[:, cols] = jnp.sum(track.astype(F32).reshape(groups, BLOCK, tile), axis=1)
            part = pl.reciprocal(above, approx=True)
            part = part * (2.0 - above * part)
            sigmoid = jnp.where(logits >= 0.0, part, decay * part)
            term[:, cols] = (cot[:, cols].astype(F32) * sigmoid).astype(BF)
        for r, ref in ((2, o2), (1, o1), (3, o3), (0, o0)):
            ref[...] = times_t(term[...], weight[slot(place, r, width), :]).astype(ref.dtype)
        done[...] = jnp.zeros_like(done)

    block = (size, width)
    return call(
        body,
        place,
        local(blocks + [head_weight, head_cot]),
        [like((size, wide), BF), like((groups, wide), F32), like(block, F32)] + [like(block, BF)] * 3 + [like((8, 128), F32)],
        scratch=[pltpu.VMEM((size, tall), BF), pltpu.VMEM((size, wide), BF)],
        after=after,
        flops=4 * size * tall * wide,
        moved=2 * tall * wide,
    )


EXTRA = 16


def add_up(place, own, came, sums, after):
    size, width = own.shape
    groups, wide = sums.shape

    def body(place, own, c1, c2, c3, sums, total, low, long, below):
        value = own[...] + c1[...].astype(F32) + c2[...].astype(F32) + c3[...].astype(F32)
        total[...] = value
        low[...] = value.astype(BF)
        long[:size, :] = value.astype(BF)
        below[...] = jnp.zeros((EXTRA, width), F32)
        for i in range(TAPS):
            cols = min(width, wide - i * width)
            below[i * groups : (i + 1) * groups, :cols] = sums[:, i * width : i * width + cols]
        long[size:, :] = below[...].astype(BF)

    return call(
        body,
        place,
        local([own] + came + [sums]),
        [like((size, width), F32), like((size, width), BF), like((size + EXTRA, width), BF)],
        scratch=[pltpu.VMEM((EXTRA, width), F32)],
        after=after,
        flops=4 * own.size,
        limit=4,
        moved=16 * own.size,
    )


def back_products(place, around, conv_weight, after):
    size, width = around[0].shape
    tall = NX * width
    cols = TAPS * width

    def body(place, d0, d1, d2, weight, o0, o1, o2, o3, done):
        for r, ref in ((2, o2), (1, o1), (3, o3), (0, o0)):
            at = slot(place, r, width)
            total = times_t(d0[...], weight[0, 0, at, :])
            total += times_t(d1[...], weight[0, 1, at, :])
            total += times_t(d2[...], weight[0, 2, at, :])
            ref[...] = total.astype(ref.dtype)
        done[...] = jnp.zeros_like(done)

    block = (size, width)
    return call(
        body,
        place,
        local(around + [conv_weight]),
        [like(block, F32)] + [like(block, BF)] * 3 + [like((8, 128), F32)],
        after=after,
        flops=2 * size * tall * cols,
        moved=2 * tall * cols,
    )


def kernel_terms(place, earlier, own, later, cots, groups, after):
    width, size = own.shape[0], own.shape[1] // NY
    half = width // 2
    cols = TAPS * width

    def body(place, earlier, own, later, d0, d1, d2, d3, kept, sent, cover, done, below, joined):
        y, z, core = place[1], place[2], place[3]
        first, last = z == 0, z == NZ - 1
        done[...] = jnp.zeros_like(done)
        for k, left in enumerate((earlier, own, later)):
            for m, right in enumerate((d0, d1, d2, d3)):
                if k == 0:
                    index = jnp.where(first, (m + 1) % NY, m)
                    valid = jnp.logical_not(jnp.logical_and(first, y == m))
                elif k == 2:
                    index = jnp.where(last, (m + NY - 1) % NY, m)
                    valid = jnp.logical_not(jnp.logical_and(last, y == (m + NY - 1) % NY))
                else:
                    joined[k, m * size : (m + 1) * size, :] = right[:size, :]
                    continue
                at = pl.ds(pl.multiple_of(index * size, size), size)

                @pl.when(valid)
                def _():
                    joined[k, at, :] = right[:size, :]

                @pl.when(jnp.logical_not(valid))
                def _():
                    joined[k, at, :] = jnp.zeros((size, width), BF)

        for k, left in enumerate((earlier, own, later)):
            total = jnp.dot(left[...], joined[k], preferred_element_type=F32)
            pairs = total.reshape(half // GROUP, 2, GROUP, width)
            one, two = (pairs[:, i].reshape(half, width) for i in range(2))
            at = slice(k * width, (k + 1) * width)
            kept[:, at] = jnp.where(core == 0, one, two)
            sent[:, at] = jnp.where(core == 0, two, one).astype(BF)
        for m, right in enumerate((d0, d1, d2, d3)):
            below[...] = right[size:, :].astype(F32)
            for i in range(TAPS):
                cover[m * groups : (m + 1) * groups, i * width : (i + 1) * width] = below[
                    i * groups : (i + 1) * groups, :
                ]

    return call(
        body,
        place,
        local([earlier, own, later] + cots),
        [like((half, cols), F32), like((half, cols), BF), like((NY * groups, cols), F32), like((8, 128), F32)],
        scratch=[pltpu.VMEM((EXTRA, width), F32), pltpu.VMEM((TAPS, NY * size, width), BF)],
        after=after,
        flops=2 * size * NY * width * cols,
        moved=8 * NY * width * size,
    )


def over_z(place, kept, came, cover, after):
    rows, cols = kept.shape

    def body(place, kept, came, cover, out, message):
        total = kept[...] + came[...].astype(F32)
        message[:EXTRA, :] = cover[...]
        for z in range(NZ):
            message[EXTRA:, :] = total[z * GROUP : (z + 1) * GROUP, :]
            out[z] = message[...].astype(BF)

    return call(
        body,
        place,
        local([kept, came, cover]),
        [like((NZ, EXTRA + GROUP, cols), BF)],
        scratch=[pltpu.VMEM((EXTRA + GROUP, cols), F32)],
        after=after,
        flops=4 * rows * cols,
        moved=6 * rows * cols,
        limit=8,
    )[0]


def summed(place, parts, wide, after):
    _, rows, cols = parts.shape
    rows = rows - EXTRA
    width = cols // TAPS

    def body(place, parts, out, blocks):
        total = jnp.zeros((rows, cols), F32)
        for z in range(NZ):
            total += parts[z].astype(F32)[EXTRA:]
            blocks[z] = parts[z, :EXTRA, :wide]
        for k in range(TAPS):
            out[k] = total[:, k * width : (k + 1) * width]

    return call(
        body,
        place,
        local([parts]),
        [like((TAPS, rows, width), F32), like((NZ, EXTRA, wide), BF)],
        after=after,
        flops=NZ * rows * cols,
        moved=2 * NZ * (rows + EXTRA) * cols,
        limit=8,
    )


def input_gradient(place, inputs, grad, own, came, after):
    def body(place, state, grad, own, c1, c2, c3, out, done):
        back_u = own[...] + c1[...].astype(F32) + c2[...].astype(F32) + c3[...].astype(F32)
        out[...] = (grad[...] + activation_slope(state[...].astype(F32), back_u)).astype(BF)
        done[...] = jnp.zeros_like(done)

    return call(
        body,
        place,
        local([inputs, grad, own] + came),
        [like(inputs.shape, BF), like((8, 128), F32)],
        after=after,
        flops=20 * inputs.size,
        limit=4,
        moved=16 * inputs.size,
    )


def counts_of(place, exon_blocks, own):
    y, core = place[1], place[3]
    flip, dz, dy, part = jnp.meshgrid(
        *(jnp.arange(n, dtype=jnp.int32) for n in (2, NZ, NY, own)), indexing="ij"
    )
    labels = seq_index((y + NY - dy) % NY, dz, core ^ flip) * own + part
    labels = labels.reshape(-1)
    return (exon_blocks[:, :, None] == labels[None, None]).astype(F32).sum(axis=1).astype(BF)


def coverage_of(blocks, counts):
    blocks = blocks.reshape(counts.shape[1], -1)
    total = jnp.dot(counts, blocks, preferred_element_type=F32)
    return total / jnp.sqrt(F32(EXONS * BLOCK))


def shards(inputs, conv_weight, head_weight, head_cot, exon_blocks):
    size, width = inputs.shape
    wide = head_cot.shape[1]
    own = size // BLOCK
    x = lax.axis_index("chan")
    s = lax.axis_index("seq")
    core, z, y = s % 2, (s // 2) % NZ, s // (2 * NZ)
    place = jnp.stack([x, y, z, core]).astype(jnp.int32)
    steps = 2

    state = inputs.astype(F32)
    acted = from_all_x(jax.nn.gelu(state).astype(BF))
    counts = counts_of(place, exon_blocks, own)
    (taps,) = load(place, [conv_weight], (token(acted[0]), counts))
    low, mid, up, whole = conv_products(place, acted, taps, ())
    low, up = shifted(low, steps), shifted(up, -steps)
    after_conv = (state + (mid + low.astype(F32) + up.astype(F32))).astype(BF)
    full = from_all_x(after_conv)
    turned = turned_blocks(place, whole, (token(after_conv),))
    turned = [turned[0]] + [along_seq(turned[m], m, 0, 0) for m in range(1, NY)]

    head, cot = load(place, [head_weight, head_cot], (token(after_conv),))
    tracks, sums, *blocks, done = track_head(place, full, head, cot, ())
    turned = stacked(place, turned, (done,))
    before = along_seq(turned, 0, 1, 0)
    behind = along_seq(turned, 0, NZ - 1, 0)
    came = [along_x(blocks[r], r) for r in range(1, NX)]
    (taps,) = load(place, [conv_weight], (done,))
    grad, low, long = add_up(place, blocks[0], came, sums, ())

    cots = [long] + [along_seq(long, m, 0, 0) for m in range(1, NY)]
    around = [shifted(low, -steps), low, shifted(low, steps)]
    kept, sent, cover, done = kernel_terms(place, before, turned, behind, cots, own, ())
    *blocks, done = back_products(place, around, taps, (done,))
    came = [along_x(blocks[r], r) for r in range(1, NX)]
    parts = over_z(place, kept, along_seq(sent, 0, 0, 1), cover, (token(came[0]),))
    groups = [[seq_index(j, i, c) for i in range(NZ)] for j in range(NY) for c in range(2)]
    parts = lax.all_to_all(parts, "seq", 0, 0, axis_index_groups=groups)
    out, done = input_gradient(place, inputs, grad, blocks[0], came, ())
    kernel_gradient, cover = summed(place, parts, wide, (done,))
    cover = jnp.stack([cover, along_seq(cover, 0, 0, 1)])
    coverage = coverage_of(cover, counts)
    return (tracks, coverage, out, kernel_gradient[None])


def solution(mesh):
    return jax.shard_map(
        shards,
        mesh=mesh,
        in_specs=(
            P("seq", "chan"),
            P(None, None, None, "chan"),
            P(None, "chan"),
            P("seq", "chan"),
            P("seq", None),
        ),
        out_specs=(
            P("seq", "chan"),
            P("seq", "chan"),
            P("seq", "chan"),
            P(None, None, "seq", "chan"),
        ),
        check_vma=False,
    )
```
